512 devices in a mesh: row: 16 (over z_lo, x), col: 16 (over y, z_hi), cond: 2 (over core).
Axes of the slice: x: 4, y: 8, z: 8 (z_hi: 2, z_lo: 4; z = z_hi * 4 + z_lo), core: 2. Of those that a mesh axis runs over, the one named last changes fastest.
Arguments:
- mask: float32 [2048, 2048], P('row', 'col'), may hold values from -1 to 1
- target: int32 [2048, 2048], P('row', 'col'), may hold values 0 or 1
- cond_index: int32 [4], P('cond'), may hold values from 0 to 7
- kernels: float32 [8, 2, 12, 576], replicated, may hold values from -6 to 6
- dose: float32 [8], replicated, may hold values from 0.7 to 1.4
Outputs:
- mask_grad: float32 [2048, 2048], P('row', 'col')
The draws below stay inside these ranges and needn't reach their ends.
All inputs are finite; a program needn't handle non-finite values. No bound on the sum of `target` on one device may be relied on, other than what follows from the above.
Results may differ from the reference program's by a relative error of at most 0.0003.
Values sent between devices are 32-bit elements; how exact they have to be, the bound alone decides.
A program may use at most 64 MiB of HBM per device.

```python
import math
import jax
import jax.numpy as jnp
from jax import lax

TILE = 128
MARGIN = 128
KERNELS = 12
CONDS = 4
SETTINGS = 8
BAND = 24
NR = 2048
NC = 2048
N_ROW = 16
N_COL = 16


def plant(entries, own_key, smallest, high):
    index_at = [jax.random.randint(jax.random.fold_in(own_key, axis), (), 0, length) for axis, length in enumerate(entries.shape)]
    widest = entries.shape.index(max(entries.shape))
    neighbour = index_at[:widest] + [(index_at[widest] + 1) % entries.shape[widest]] + index_at[widest + 1:]
    return entries.at[tuple(index_at)].set(smallest).at[tuple(neighbour)].set(high)


def shard_levels(key, shape, pieces, low, top_value):
    def one(axis_at, parts):
        steps = jax.random.uniform(jax.random.fold_in(jax.random.fold_in(key, 6), axis_at), (parts,), jnp.float32, low / len(pieces), top_value / len(pieces))
        return jnp.repeat(jnp.exp(steps), shape[axis_at] // parts).reshape((-1,) + (1,) * (len(shape) - axis_at - 1))

    factor_of = one(*pieces[0])
    for cut in pieces[1:]:
        factor_of = factor_of * one(*cut)
    return factor_of


def centred(key, dims, spread, bound, held_as=jnp.bfloat16):
    values = spread * jax.random.normal(key, dims, jnp.float32)
    return jnp.clip(values, min=-bound, max=bound).astype(held_as)


def setup_inputs(seed: int = 0) -> dict:
    arg_keys = jax.random.split(jax.random.key(seed), 6)
    return {
        "mask": jnp.clip(jax.random.uniform(arg_keys[0], (NR, NC), jnp.float32, -1.0, 1.0) * shard_levels(arg_keys[0], (NR, NC), ((0, 16), (1, 16)), -0.4, 0.0), -1.0, 1.0),
        "target": plant((jax.random.randint(arg_keys[1], (NR, NC), 0, 2) < 1).astype(jnp.int32), jax.random.fold_in(arg_keys[1], 1), 0, 1),
        "cond_index": plant(jax.random.randint(arg_keys[2], (CONDS,), 0, SETTINGS), jax.random.fold_in(arg_keys[2], 1), 0, SETTINGS - 1).astype(jnp.int32),
        "kernels": centred(arg_keys[3], (SETTINGS, 2, KERNELS, BAND * BAND), 1.0, 6.0, jnp.float32),
        "dose": jnp.clip(jnp.exp(jax.random.uniform(arg_keys[4], (SETTINGS,), jnp.float32, math.log(0.7), math.log(1.4))), 0.7, 1.4),
    }


STEEP = 4.0
THRESH = 0.6

def highest(left_side, right_side):
    return jnp.dot(left_side, right_side, precision=lax.Precision.HIGHEST, preferred_element_type=jnp.float32)

def tables(length, start, window_size, band_size):
    frequency = jnp.arange(band_size, dtype=jnp.int32) - band_size // 2
    positions = jnp.arange(length, dtype=jnp.int32) + start
    phases = frequency[:, None] * positions[None, :] % window_size
    angles = phases.astype(jnp.float32) * (2.0 * math.pi / window_size)
    return (jnp.cos(angles), jnp.sin(angles))

def row_product(segment, row_start, window_size, band_size):
    cosine_table, sine_table = tables(segment.shape[0], row_start, window_size, band_size)
    return highest(jnp.concatenate([cosine_table, sine_table], axis=0), segment)

def col_product(partial_rows, col_start, window_size, band_size):
    cosine_table, sine_table = tables(partial_rows.shape[1], col_start, window_size, band_size)
    products = highest(partial_rows, jnp.concatenate([cosine_table, sine_table], axis=0).T)
    upper_cos = products[:band_size, :band_size]
    upper_sin = products[:band_size, band_size:]
    lower_cos = products[band_size:, :band_size]
    lower_sin = products[band_size:, band_size:]
    return jnp.stack([upper_cos - lower_sin, -lower_cos - upper_sin]) / window_size

def tile_loss(spectrum, kernel, dose_value, goal_map):
    tile_size = goal_map.shape[0]
    band_size = spectrum.shape[1]
    window_size = tile_size + 2 * MARGIN
    kernel_real = kernel[0].reshape(-1, band_size, band_size)
    kernel_imag = kernel[1].reshape(-1, band_size, band_size)
    kernel_count = kernel_real.shape[0]
    product_real = kernel_real * spectrum[0] - kernel_imag * spectrum[1]
    product_imag = kernel_real * spectrum[1] + kernel_imag * spectrum[0]
    stacked = jnp.concatenate([product_real, product_imag], axis=1)
    stacked = jnp.transpose(stacked, (1, 0, 2)).reshape(2 * band_size, kernel_count * band_size)
    cosine_table, sine_table = tables(tile_size, MARGIN, window_size, band_size)
    cosine_cols = cosine_table.T
    sine_cols = sine_table.T
    inverse_left = jnp.concatenate([jnp.concatenate([cosine_cols, -sine_cols], 1), jnp.concatenate([sine_cols, cosine_cols], 1)], 0)
    partial_rows = highest(inverse_left, stacked)
    rows_real = partial_rows[:tile_size].reshape(tile_size, kernel_count, band_size)
    rows_imag = partial_rows[tile_size:].reshape(tile_size, kernel_count, band_size)
    rows_both = jnp.concatenate([rows_real, rows_imag], axis=2)
    rows_both = jnp.transpose(rows_both, (1, 0, 2)).reshape(kernel_count * tile_size, 2 * band_size)
    inverse_right = jnp.concatenate([jnp.concatenate([cosine_table, sine_table], 1), jnp.concatenate([-sine_table, cosine_table], 1)], 0)
    fields = highest(rows_both, inverse_right)
    squared = (fields * fields).reshape(kernel_count, tile_size, 2, tile_size)
    intensity = lax.optimization_barrier(jnp.sum(squared, axis=(0, 2))) / (kernel_count * band_size * band_size)
    resist = jax.nn.sigmoid(STEEP * (dose_value * intensity - THRESH))
    return jnp.sum(jnp.square(resist - goal_map))

def interior_adjoint(cotangent, tile_size, window_size):
    band_size = cotangent.shape[1]
    cosine_table, sine_table = tables(tile_size, MARGIN, window_size, band_size)
    joined = jnp.concatenate([cotangent[0], cotangent[1]], axis=1)
    right_side = jnp.concatenate([jnp.concatenate([cosine_table, -sine_table], 1), jnp.concatenate([-sine_table, -cosine_table], 1)], 0)
    halves = highest(joined, right_side)
    stacked = jnp.concatenate([halves[:, :tile_size], halves[:, tile_size:]], axis=0)
    left_side = jnp.concatenate([cosine_table, sine_table], axis=0).T
    return highest(left_side, stacked) / window_size

def reference(mask, target, cond_index, kernels, dose):
    window_size = TILE + 2 * MARGIN
    padded = jnp.pad(mask, MARGIN)

    def tile_gradient(position):
        tile_row = position // N_COL
        tile_col = position % N_COL
        window = lax.dynamic_slice(padded, (tile_row * TILE, tile_col * TILE), (window_size, window_size))
        goal_map = lax.dynamic_slice(target, (tile_row * TILE, tile_col * TILE), (TILE, TILE)).astype(jnp.float32)
        spectrum = col_product(row_product(window, 0, window_size, BAND), 0, window_size, BAND)
        summed = jnp.zeros((2, BAND, BAND), jnp.float32)
        for ordinal in range(CONDS):
            setting = cond_index[ordinal]
            kernel = lax.dynamic_index_in_dim(kernels, setting, 0, keepdims=False)
            dose_value = lax.dynamic_index_in_dim(dose, setting, 0, keepdims=False)
            summed = summed + jax.grad(tile_loss)(spectrum, kernel, dose_value, goal_map)
        return interior_adjoint(summed, TILE, window_size)
    gradients = lax.map(tile_gradient, jnp.arange(N_ROW * N_COL, dtype=jnp.int32))
    return gradients.reshape(N_ROW, N_COL, TILE, TILE).transpose(0, 2, 1, 3).reshape(N_ROW * TILE, N_COL * TILE)
```

```python
import functools
import math

import jax
import jax.numpy as jnp
import ml_dtypes
import numpy as np
from jax import lax
from jax.experimental import pallas as pl
from jax.experimental.pallas import tpu as pltpu
from jax.sharding import PartitionSpec as P

MESH = pl.DeviceIdType.MESH
BF = jnp.bfloat16
F32 = jnp.float32

TILE = 128
MARGIN = 128
WINDOW = TILE + 2 * MARGIN
BAND = 24
KERNELS = 12
HALF = BAND // 2
REAL = 2 * HALF + 1
PACK = 5
GRID = 48
GROUP = 4
CONDS = 2
TILES = CONDS * KERNELS // GROUP
STEEP = 4.0
THRESH = 0.6
OFFSETS = [(-1, -1), (-1, 0), (-1, 1), (0, -1), (0, 1), (1, -1), (1, 0), (1, 1)]
FREQ = np.arange(BAND) - HALF
UNIT = 2.0 * math.pi / WINDOW


def parts(table):
    high = table.astype(ml_dtypes.bfloat16)
    low = (table - high.astype(np.float64)).astype(ml_dtypes.bfloat16)
    return high, low


def left3(table):
    high, low = parts(table)
    return np.concatenate([high, high, low], axis=1)


def pair(table):
    return np.stack(parts(table))


def real_basis(positions):
    order = np.arange(HALF + 1)[:, None] * positions[None, :] % WINDOW * UNIT
    return np.concatenate([np.cos(order), np.sin(order)[1:]], axis=0)


def make_tables():
    t = {}
    pixels = np.arange(TILE)
    rows = np.zeros((3, PACK, 8, TILE))
    cols = np.zeros((3, TILE, TILE))
    for d in range(3):
        basis = real_basis(pixels + TILE * (d - 1))
        rows[d, :, :PACK] = basis.reshape(PACK, PACK, TILE)
        for j in range(PACK):
            cols[d, :, REAL * j : REAL * (j + 1)] = basis.T / WINDOW
    t["dft_rows"] = left3(rows.reshape(3 * PACK * 8, TILE))
    t["dft_cols"] = pair(cols.transpose(1, 0, 2).reshape(TILE, 3 * TILE))
    lane_group = np.zeros((PACK, 8, TILE), np.float32)
    for j in range(PACK):
        lane_group[j, :, REAL * j : REAL * (j + 1)] = 1.0

    pick = np.zeros((PACK, BAND, 2 * TILE), np.float32)
    spread = np.zeros((2, TILE, 2, GROUP, 32))
    for row, f in enumerate(FREQ):
        a = abs(f)
        j, i = divmod(a, PACK)
        pick[i, row, REAL * j : REAL * (j + 1)] = 1.0
        if f:
            j, i = divmod(HALF + a, PACK)
            pick[i, row, TILE + REAL * j : TILE + REAL * (j + 1)] = np.sign(f)
    for j in range(PACK):
        for col, g in enumerate(FREQ):
            cos_at = REAL * j + abs(g)
            spread[0, cos_at, 0, :, col] = 1.0
            spread[1, cos_at, 1, :, col] = -1.0
            if g:
                sin_at = REAL * j + HALF + abs(g)
                spread[1, sin_at, 0, :, col] = -np.sign(g)
                spread[0, sin_at, 1, :, col] = -np.sign(g)
    t["pick"] = pick
    t["lane_group"] = lane_group
    t["spread"] = spread.reshape(2 * TILE, 2 * TILE).astype(ml_dtypes.bfloat16)

    flat = np.arange(640)
    rows_of = np.zeros((BAND, 640), np.float32)
    fold = np.zeros((640, GROUP, 32))
    for l in range(BAND * BAND):
        rows_of[l // BAND, l] = 1.0
        fold[l, :, l % BAND] = 1.0
    t["rows_of"] = rows_of[:, : BAND * BAND]
    t["fold"] = fold.reshape(640, TILE)[: BAND * BAND].astype(ml_dtypes.bfloat16)

    angle = FREQ[:, None] * np.arange(GRID)[None, :] % GRID * (2.0 * math.pi / GRID)
    c, s = np.cos(angle), np.sin(angle)
    field_rows = np.block([[c.T, -s.T], [s.T, c.T]])
    t["field_rows"] = left3(field_rows)
    t["field_rows_t"] = left3(field_rows.T)
    field_cols = np.zeros((2, GROUP, 32, 2, GROUP, 64))
    for k in range(GROUP):
        field_cols[0, k, :BAND, 0, k, :GRID] = c
        field_cols[1, k, :BAND, 0, k, :GRID] = -s
        field_cols[0, k, :BAND, 1, k, :GRID] = s
        field_cols[1, k, :BAND, 1, k, :GRID] = c
    field_cols = field_cols.reshape(2 * TILE, 4 * TILE)
    t["field_cols"] = pair(field_cols)
    t["field_cols_t"] = pair(field_cols.T.copy())

    step = WINDOW // GRID
    gap = pixels[:, None] - step * np.arange(GRID)[None, :]
    orders = np.arange(1, GRID // 2)
    inter = (1.0 + 2.0 * np.cos(orders * gap[:, :, None] * UNIT).sum(-1)) / GRID
    inter_wide = np.zeros((TILE, GROUP, 64))
    inter_wide[:, :, :GRID] = inter[:, None, :]
    inter_wide = inter_wide.reshape(TILE, 2 * TILE)
    t["inter_rows"] = left3(inter)
    t["inter_rows_t"] = left3(inter.T)
    t["inter_cols"] = pair(inter_wide.T.copy())
    t["inter_cols_t"] = pair(inter_wide)

    turn = FREQ[:, None] * pixels[None, :] % WINDOW * UNIT
    c, s = np.cos(turn), np.sin(turn)
    last_cols = np.zeros((2, GROUP, 32, 2, TILE))
    last_cols[0, :, :BAND, 0] = c / WINDOW
    last_cols[1, :, :BAND, 0] = -s / WINDOW
    last_cols[0, :, :BAND, 1] = -s / WINDOW
    last_cols[1, :, :BAND, 1] = -c / WINDOW
    t["last_cols"] = pair(last_cols.reshape(2 * TILE, 2 * TILE))
    t["last_rows"] = left3(np.concatenate([c, s], axis=0).T)
    return t


TABLES = make_tables()
NAMES = [
    "dft_rows", "dft_cols", "lane_group", "rows_of", "fold", "pick", "spread", "field_rows", "field_cols",
    "inter_cols", "inter_rows", "inter_rows_t", "inter_cols_t", "field_cols_t", "field_rows_t", "last_cols",
]


def split(x):
    high = x.astype(BF)
    return high, (x - high.astype(F32)).astype(BF)


def dot(a, b):
    return jnp.dot(a, b, preferred_element_type=F32)


def dot3(x, table):
    high, low = split(x)
    return dot(high, table[0]) + dot(low, table[0]) + dot(high, table[1])


def stacked3(x):
    high, low = split(x)
    return jnp.concatenate([high, low, high], axis=0)


def main_kernel(*refs):
    n = len(NAMES)
    mask_hbm, target_hbm, kernels_hbm, cond_ref, dose_ref = refs[:5]
    tables_hbm = refs[5 : 5 + n]
    out_ref = refs[5 + n]
    scratch = refs[6 + n :]
    tab = dict(zip(NAMES, scratch[:n]))
    mask, target, kernels, kk, sent, held, swap, load_sem, send_sem, recv_sem = scratch[n:]

    row, col, core = (lax.axis_index(a) for a in ("row", "col", "cond"))
    n_row, n_col = lax.axis_size("row"), lax.axis_size("col")

    copies = {}
    for i, (name, src, dst) in enumerate(
        [("mask", mask_hbm, mask)]
        + [(m, s, tab[m]) for m, s in zip(NAMES[:3], tables_hbm[:3])]
        + [("kernels", kernels_hbm, kernels)]
        + [(m, s, tab[m]) for m, s in zip(NAMES[3:], tables_hbm[3:])]
        + [("target", target_hbm, target)]
    ):
        copies[name] = pltpu.make_async_copy(src, dst, load_sem.at[i])
        copies[name].start()

    held[...] = jnp.zeros_like(held)
    barrier = pltpu.get_barrier_semaphore()
    count = jnp.int32(1)
    pl.semaphore_signal(barrier, inc=1, device_id=(row, col, 1 - core), device_id_type=MESH)
    there = []
    for dr, dc in OFFSETS:
        ok = (row + dr >= 0) & (row + dr < n_row) & (col + dc >= 0) & (col + dc < n_col)
        there.append(ok)
        count = count + ok.astype(jnp.int32)

        @pl.when(ok)
        def _():
            pl.semaphore_signal(barrier, inc=1, device_id=(row + dr, col + dc, core), device_id_type=MESH)

    for name in ("mask", "dft_rows", "dft_cols", "lane_group"):
        copies[name].wait()
    partial = dot(tab["dft_rows"][...], stacked3(mask[...]))
    blocks = dot3(partial, tab["dft_cols"])
    own = None
    at = 0
    for d in range(3):
        for e in range(3):
            block = None
            for j in range(PACK):
                piece = blocks[8 * (PACK * d + j) : 8 * (PACK * d + j + 1), TILE * e : TILE * (e + 1)]
                piece = piece * tab["lane_group"][j]
                block = piece if block is None else block + piece
            if d == 1 and e == 1:
                own = block
            else:
                sent[at] = block[:PACK]
                at += 1

    pl.semaphore_wait(barrier, count)
    sends = []
    for i, (dr, dc) in enumerate(OFFSETS):
        copy = pltpu.make_async_remote_copy(
            src_ref=sent.at[i],
            dst_ref=held.at[i],
            send_sem=send_sem.at[i],
            recv_sem=recv_sem.at[i],
            device_id=(row - dr, col - dc, core),
            device_id_type=MESH,
        )
        sends.append(copy)

        @pl.when(there[len(OFFSETS) - 1 - i])
        def _(copy=copy):
            copy.start()

    for name in ("kernels", "rows_of", "fold"):
        copies[name].wait()
    lane = lax.broadcasted_iota(jnp.int32, (BAND, TILE), 1) // 32

    def arrange(step, carry):
        c = step // 3
        group = step - 3 * c
        setting = cond_ref[c]
        for part in range(2):
            total = jnp.zeros((BAND, TILE), F32)
            for k in range(GROUP):
                line = kernels[setting, part, pl.ds(group * GROUP + k, 1), :]
                high, low = split(line * tab["rows_of"][...])
                folded = dot(high, tab["fold"][...]) + dot(low, tab["fold"][...])
                total = total + jnp.where(lane == k, folded, 0.0)
            kk[part, step] = total
        return carry

    lax.fori_loop(0, TILES, arrange, 0)
    for name in NAMES[5:] + ["target"]:
        copies[name].wait()
    doses = [dose_ref[cond_ref[c]] for c in range(CONDS)]
    goal = target[...].astype(F32)

    for i in range(len(OFFSETS)):

        @pl.when(there[i])
        def _(i=i):
            sends[i].wait_recv()

    z = own[:PACK]
    for i in range(len(OFFSETS)):
        z = z + held[i]
    chosen = None
    for i in range(PACK):
        line = jnp.concatenate([z[i : i + 1], z[i : i + 1]], axis=1)
        piece = line * tab["pick"][i]
        chosen = piece if chosen is None else chosen + piece
    high, low = split(chosen)
    spectrum = dot(high, tab["spread"][...]) + dot(low, tab["spread"][...])
    s_re, s_im = spectrum[:, :TILE], spectrum[:, TILE:]
    product = []
    for j in range(TILES):
        k_re, k_im = kk[0, j], kk[1, j]
        product.append(jnp.concatenate([k_re * s_re - k_im * s_im, k_re * s_im + k_im * s_re], axis=0))
    along = dot(tab["field_rows"][...], stacked3(jnp.concatenate(product, axis=1)))
    along = jnp.concatenate(
        [
            jnp.concatenate([along[:GRID, TILE * j : TILE * (j + 1)], along[GRID:, TILE * j : TILE * (j + 1)]], axis=1)
            for j in range(TILES)
        ],
        axis=0,
    )
    field = dot3(along, tab["field_cols"])
    square = field * field
    square = square[:, : 2 * TILE] + square[:, 2 * TILE :]
    samples = []
    for c in range(CONDS):
        at = c * (TILES // CONDS) * GRID
        samples.append(square[at : at + GRID] + square[at + GRID : at + 2 * GRID] + square[at + 2 * GRID : at + 3 * GRID])
    inten = dot3(jnp.concatenate(samples, axis=0), tab["inter_cols"])
    inten = jnp.concatenate([inten[:GRID], inten[GRID:]], axis=1)
    inten = dot(tab["inter_rows"][...], stacked3(inten))
    slopes = []
    for c in range(CONDS):
        scale = doses[c] * (STEEP / (KERNELS * BAND * BAND))
        arg = scale * inten[:, TILE * c : TILE * (c + 1)] - STEEP * THRESH
        e = jnp.exp(-jnp.abs(arg))
        inverse = 1.0 / (1.0 + e)
        resist = jnp.where(arg >= 0, inverse, e * inverse)
        slopes.append((resist - goal) * (e * inverse * inverse) * (4.0 * scale))
    back = dot(tab["inter_rows_t"][...], stacked3(jnp.concatenate(slopes, axis=1)))
    back = jnp.concatenate([back[:, :TILE], back[:, TILE:]], axis=0)
    weight = dot3(back, tab["inter_cols_t"])
    pulled = []
    for j in range(TILES):
        at = j // (TILES // CONDS) * GRID
        w = weight[at : at + GRID]
        pulled.append(field[GRID * j : GRID * (j + 1)] * jnp.concatenate([w, w], axis=1))
    pulled = dot3(jnp.concatenate(pulled, axis=0), tab["field_cols_t"])
    pulled = jnp.concatenate(
        [
            jnp.concatenate([pulled[GRID * j : GRID * (j + 1), TILE * p : TILE * (p + 1)] for j in range(TILES)], axis=1)
            for p in range(2)
        ],
        axis=0,
    )
    pulled = dot(tab["field_rows_t"][...], stacked3(pulled))
    d_re = d_im = None
    for j in range(TILES):
        k_re, k_im = kk[0, j], kk[1, j]
        p_re = pulled[:BAND, TILE * j : TILE * (j + 1)]
        p_im = pulled[BAND:, TILE * j : TILE * (j + 1)]
        re, im = k_re * p_re + k_im * p_im, k_re * p_im - k_im * p_re
        d_re, d_im = (re, im) if d_re is None else (d_re + re, d_im + im)
    last = dot3(jnp.concatenate([d_re, d_im], axis=1), tab["last_cols"])
    swap[0, :BAND] = last[:, :TILE]
    swap[0, BAND:] = last[:, TILE:]
    copy = pltpu.make_async_remote_copy(
        src_ref=swap.at[0],
        dst_ref=swap.at[1],
        send_sem=send_sem.at[len(OFFSETS)],
        recv_sem=recv_sem.at[len(OFFSETS)],
        device_id=(row, col, 1 - core),
        device_id_type=MESH,
    )
    copy.start()
    for i in range(len(OFFSETS)):

        @pl.when(there[len(OFFSETS) - 1 - i])
        def _(i=i):
            sends[i].wait_send()

    copy.wait()
    out_ref[...] = swap[0] + swap[1]


def last_kernel(table_ref, sums_ref, out_ref):
    out_ref[...] = dot(table_ref[...], stacked3(sums_ref[...]))


def shards(mask, target, cond_index, kernels, dose):
    any_spec = pl.BlockSpec(memory_space=pl.ANY)
    smem = pl.BlockSpec(memory_space=pltpu.SMEM)
    vmem = pl.BlockSpec(memory_space=pltpu.VMEM)
    tables = [jnp.asarray(TABLES[name]) for name in NAMES]
    sums = pl.pallas_call(
        main_kernel,
        out_shape=jax.ShapeDtypeStruct((2 * BAND, TILE), F32),
        in_specs=[any_spec, any_spec, any_spec, smem, smem] + [any_spec] * len(tables),
        out_specs=vmem,
        scratch_shapes=[pltpu.VMEM(x.shape, x.dtype) for x in tables]
        + [
            pltpu.VMEM(mask.shape, F32),
            pltpu.VMEM(target.shape, jnp.int32),
            pltpu.VMEM(kernels.shape, F32),
            pltpu.VMEM((2, TILES, BAND, TILE), F32),
            pltpu.VMEM((len(OFFSETS), PACK, TILE), F32),
            pltpu.VMEM((len(OFFSETS), PACK, TILE), F32),
            pltpu.VMEM((2, 2 * BAND, TILE), F32),
            pltpu.SemaphoreType.DMA((len(tables) + 3,)),
            pltpu.SemaphoreType.DMA((len(OFFSETS) + 1,)),
            pltpu.SemaphoreType.DMA((len(OFFSETS) + 1,)),
        ],
        compiler_params=pltpu.CompilerParams(
            collective_id=0, has_side_effects=True, vmem_limit_bytes=48 * 1024 * 1024
        ),
        name="spectra_and_gradient",
    )(mask, target, kernels, cond_index, dose, *tables)
    return pl.pallas_call(
        last_kernel,
        out_shape=jax.ShapeDtypeStruct(mask.shape, F32),
        in_specs=[vmem, vmem],
        out_specs=vmem,
        name="to_pixels",
    )(jnp.asarray(TABLES["last_rows"]), sums)


def solution(mesh):
    in_specs = (P("row", "col"), P("row", "col"), P("cond"), P(), P())
    out_specs = P("row", "col")
    return jax.shard_map(shards, mesh=mesh, in_specs=in_specs, out_specs=out_specs, check_vma=False)
```

```python
import functools
import math

import jax
import jax.numpy as jnp
import ml_dtypes
import numpy as np
from jax import lax
from jax.experimental import pallas as pl
from jax.experimental.pallas import tpu as pltpu
from jax.sharding import PartitionSpec as P

MESH = pl.DeviceIdType.MESH
BF = jnp.bfloat16
F32 = jnp.float32

TILE = 128
MARGIN = 128
WINDOW = TILE + 2 * MARGIN
BAND = 24
KERNELS = 12
HALF = BAND // 2
REAL = 2 * HALF + 1
PACK = 5
GRID = 48
GROUP = 4
CONDS = 2
TILES = CONDS * KERNELS // GROUP
STEEP = 4.0
THRESH = 0.6
OFFSETS = [(-1, -1), (-1, 0), (-1, 1), (0, -1), (0, 1), (1, -1), (1, 0), (1, 1)]
FREQ = np.arange(BAND) - HALF
UNIT = 2.0 * math.pi / WINDOW


def parts(table):
    high = table.astype(ml_dtypes.bfloat16)
    low = (table - high.astype(np.float64)).astype(ml_dtypes.bfloat16)
    return high, low


def left3(table):
    high, low = parts(table)
    return np.concatenate([high, high, low], axis=1)


def pair(table):
    return np.stack(parts(table))


def real_basis(positions):
    order = np.arange(HALF + 1)[:, None] * positions[None, :] % WINDOW * UNIT
    return np.concatenate([np.cos(order), np.sin(order)[1:]], axis=0)


def make_tables():
    t = {}
    pixels = np.arange(TILE)
    rows = np.zeros((3, PACK, 8, TILE))
    cols = np.zeros((3, TILE, TILE))
    for d in range(3):
        basis = real_basis(pixels + TILE * (d - 1))
        rows[d, :, :PACK] = basis.reshape(PACK, PACK, TILE)
        for j in range(PACK):
            cols[d, :, REAL * j : REAL * (j + 1)] = basis.T / WINDOW
    t["dft_rows"] = left3(rows.reshape(3 * PACK * 8, TILE))
    t["dft_cols"] = pair(cols.transpose(1, 0, 2).reshape(TILE, 3 * TILE))
    lane_group = np.zeros((PACK, 8, TILE), np.float32)
    for j in range(PACK):
        lane_group[j, :, REAL * j : REAL * (j + 1)] = 1.0

    pick = np.zeros((PACK, BAND, 2 * TILE), np.float32)
    spread = np.zeros((2, TILE, 2, GROUP, 32))
    for row, f in enumerate(FREQ):
        a = abs(f)
        j, i = divmod(a, PACK)
        pick[i, row, REAL * j : REAL * (j + 1)] = 1.0
        if f:
            j, i = divmod(HALF + a, PACK)
            pick[i, row, TILE + REAL * j : TILE + REAL * (j + 1)] = np.sign(f)
    for j in range(PACK):
        for col, g in enumerate(FREQ):
            cos_at = REAL * j + abs(g)
            spread[0, cos_at, 0, :, col] = 1.0
            spread[1, cos_at, 1, :, col] = -1.0
            if g:
                sin_at = REAL * j + HALF + abs(g)
                spread[1, sin_at, 0, :, col] = -np.sign(g)
                spread[0, sin_at, 1, :, col] = -np.sign(g)
    t["pick"] = pick
    t["lane_group"] = lane_group
    t["spread"] = spread.reshape(2 * TILE, 2 * TILE).astype(ml_dtypes.bfloat16)

    flat = np.arange(640)
    rows_of = np.zeros((BAND, 640), np.float32)
    fold = np.zeros((640, GROUP, 32))
    for l in range(BAND * BAND):
        rows_of[l // BAND, l] = 1.0
        fold[l, :, l % BAND] = 1.0
    t["rows_of"] = rows_of[:, : BAND * BAND]
    t["fold"] = fold.reshape(640, TILE)[: BAND * BAND].astype(ml_dtypes.bfloat16)

    angle = FREQ[:, None] * np.arange(GRID)[None, :] % GRID * (2.0 * math.pi / GRID)
    c, s = np.cos(angle), np.sin(angle)
    field_rows = np.block([[c.T, -s.T], [s.T, c.T]])
    t["field_rows"] = left3(field_rows)
    t["field_rows_t"] = left3(field_rows.T)
    field_cols = np.zeros((2, GROUP, 32, 2, GROUP, 64))
    for k in range(GROUP):
        field_cols[0, k, :BAND, 0, k, :GRID] = c
        field_cols[1, k, :BAND, 0, k, :GRID] = -s
        field_cols[0, k, :BAND, 1, k, :GRID] = s
        field_cols[1, k, :BAND, 1, k, :GRID] = c
    field_cols = field_cols.reshape(2 * TILE, 4 * TILE)
    t["field_cols"] = pair(field_cols)
    t["field_cols_t"] = pair(field_cols.T.copy())

    step = WINDOW // GRID
    gap = pixels[:, None] - step * np.arange(GRID)[None, :]
    orders = np.arange(1, GRID // 2)
    inter = (1.0 + 2.0 * np.cos(orders * gap[:, :, None] * UNIT).sum(-1)) / GRID
    inter_wide = np.zeros((TILE, GROUP, 64))
    inter_wide[:, :, :GRID] = inter[:, None, :]
    inter_wide = inter_wide.reshape(TILE, 2 * TILE)
    t["inter_rows"] = left3(inter)
    t["inter_rows_t"] = left3(inter.T)
    t["inter_cols"] = pair(inter_wide.T.copy())
    t["inter_cols_t"] = pair(inter_wide)

    turn = FREQ[:, None] * pixels[None, :] % WINDOW * UNIT
    c, s = np.cos(turn), np.sin(turn)
    last_cols = np.zeros((2, GROUP, 32, 2, TILE))
    last_cols[0, :, :BAND, 0] = c / WINDOW
    last_cols[1, :, :BAND, 0] = -s / WINDOW
    last_cols[0, :, :BAND, 1] = -s / WINDOW
    last_cols[1, :, :BAND, 1] = -c / WINDOW
    t["last_cols"] = pair(last_cols.reshape(2 * TILE, 2 * TILE))
    t["last_rows"] = left3(np.concatenate([c, s], axis=0).T)
    return t


TABLES = make_tables()
NAMES = [
    "dft_rows", "dft_cols", "lane_group", "rows_of", "fold", "pick", "spread", "field_rows", "field_cols",
    "inter_cols", "inter_rows", "inter_rows_t", "inter_cols_t", "field_cols_t", "field_rows_t", "last_cols",
]


def split(x):
    high = x.astype(BF)
    return high, (x - high.astype(F32)).astype(BF)


def dot(a, b):
    return jnp.dot(a, b, preferred_element_type=F32)


def dot3(x, table):
    high, low = split(x)
    return dot(high, table[0]) + dot(low, table[0]) + dot(high, table[1])


def stacked3(x):
    high, low = split(x)
    return jnp.concatenate([high, low, high], axis=0)


def main_kernel(*refs):
    n = len(NAMES)
    mask_hbm, target_hbm, kernels_hbm, cond_hbm, dose_hbm = refs[:5]
    tables_hbm = refs[5 : 5 + n]
    out_ref = refs[5 + n]
    scratch = refs[6 + n :]
    tab = dict(zip(NAMES, scratch[:n]))
    mask, target, kernels, cond_ref, dose_ref, kk, sent, held, swap, load_sem, send_sem, recv_sem = scratch[n:]

    row, col, core = (lax.axis_index(a) for a in ("row", "col", "cond"))
    n_row, n_col = lax.axis_size("row"), lax.axis_size("col")

    copies = {}
    for i, (name, src, dst) in enumerate(
        [("mask", mask_hbm, mask)]
        + [(m, s, tab[m]) for m, s in zip(NAMES[:3], tables_hbm[:3])]
        + [("kernels", kernels_hbm, kernels), ("cond", cond_hbm, cond_ref), ("dose", dose_hbm, dose_ref)]
        + [(m, s, tab[m]) for m, s in zip(NAMES[3:], tables_hbm[3:])]
        + [("target", target_hbm, target)]
    ):
        copies[name] = pltpu.make_async_copy(src, dst, load_sem.at[i])
        copies[name].start()

    held[...] = jnp.zeros_like(held)
    barrier = pltpu.get_barrier_semaphore()
    count = jnp.int32(1)
    pl.semaphore_signal(barrier, inc=1, device_id=(row, col, 1 - core), device_id_type=MESH)
    there = []
    for dr, dc in OFFSETS:
        ok = (row + dr >= 0) & (row + dr < n_row) & (col + dc >= 0) & (col + dc < n_col)
        there.append(ok)
        count = count + ok.astype(jnp.int32)

        @pl.when(ok)
        def _():
            pl.semaphore_signal(barrier, inc=1, device_id=(row + dr, col + dc, core), device_id_type=MESH)

    for name in ("mask", "dft_rows", "dft_cols", "lane_group"):
        copies[name].wait()
    partial = dot(tab["dft_rows"][...], stacked3(mask[...]))
    blocks = dot3(partial, tab["dft_cols"])
    own = None
    at = 0
    for d in range(3):
        for e in range(3):
            block = None
            for j in range(PACK):
                piece = blocks[8 * (PACK * d + j) : 8 * (PACK * d + j + 1), TILE * e : TILE * (e + 1)]
                piece = piece * tab["lane_group"][j]
                block = piece if block is None else block + piece
            if d == 1 and e == 1:
                own = block
            else:
                sent[at] = block[:PACK]
                at += 1

    pl.semaphore_wait(barrier, count)
    sends = []
    for i, (dr, dc) in enumerate(OFFSETS):
        copy = pltpu.make_async_remote_copy(
            src_ref=sent.at[i],
            dst_ref=held.at[i],
            send_sem=send_sem.at[i],
            recv_sem=recv_sem.at[i],
            device_id=(row - dr, col - dc, core),
            device_id_type=MESH,
        )
        sends.append(copy)

        @pl.when(there[len(OFFSETS) - 1 - i])
        def _(copy=copy):
            copy.start()

    for name in ("kernels", "cond", "dose", "rows_of", "fold"):
        copies[name].wait()
    lane = lax.broadcasted_iota(jnp.int32, (BAND, TILE), 1) // 32

    def arrange(step, carry):
        c = step // 3
        group = step - 3 * c
        setting = cond_ref[c]
        for part in range(2):
            total = jnp.zeros((BAND, TILE), F32)
            for k in range(GROUP):
                line = kernels[setting, group * GROUP + k, part : part + 1, :]
                high, low = split(line * tab["rows_of"][...])
                folded = dot(high, tab["fold"][...]) + dot(low, tab["fold"][...])
                total = total + jnp.where(lane == k, folded, 0.0)
            kk[part, step] = total
        return carry

    lax.fori_loop(0, TILES, arrange, 0)
    for name in NAMES[5:] + ["target"]:
        copies[name].wait()
    doses = [dose_ref[cond_ref[c]] for c in range(CONDS)]
    goal = target[...].astype(F32)

    for i in range(len(OFFSETS)):

        @pl.when(there[i])
        def _(i=i):
            sends[i].wait_recv()

    z = own[:PACK]
    for i in range(len(OFFSETS)):
        z = z + held[i]
    chosen = None
    for i in range(PACK):
        line = jnp.concatenate([z[i : i + 1], z[i : i + 1]], axis=1)
        piece = line * tab["pick"][i]
        chosen = piece if chosen is None else chosen + piece
    high, low = split(chosen)
    spectrum = dot(high, tab["spread"][...]) + dot(low, tab["spread"][...])
    s_re, s_im = spectrum[:, :TILE], spectrum[:, TILE:]
    product = []
    for j in range(TILES):
        k_re, k_im = kk[0, j], kk[1, j]
        product.append(jnp.concatenate([k_re * s_re - k_im * s_im, k_re * s_im + k_im * s_re], axis=0))
    along = dot(tab["field_rows"][...], stacked3(jnp.concatenate(product, axis=1)))
    along = jnp.concatenate(
        [
            jnp.concatenate([along[:GRID, TILE * j : TILE * (j + 1)], along[GRID:, TILE * j : TILE * (j + 1)]], axis=1)
            for j in range(TILES)
        ],
        axis=0,
    )
    field = dot3(along, tab["field_cols"])
    square = field * field
    square = square[:, : 2 * TILE] + square[:, 2 * TILE :]
    samples = []
    for c in range(CONDS):
        at = c * (TILES // CONDS) * GRID
        samples.append(square[at : at + GRID] + square[at + GRID : at + 2 * GRID] + square[at + 2 * GRID : at + 3 * GRID])
    inten = dot3(jnp.concatenate(samples, axis=0), tab["inter_cols"])
    inten = jnp.concatenate([inten[:GRID], inten[GRID:]], axis=1)
    inten = dot(tab["inter_rows"][...], stacked3(inten))
    slopes = []
    for c in range(CONDS):
        scale = doses[c] * (STEEP / (KERNELS * BAND * BAND))
        arg = scale * inten[:, TILE * c : TILE * (c + 1)] - STEEP * THRESH
        e = jnp.exp(-jnp.abs(arg))
        inverse = 1.0 / (1.0 + e)
        resist = jnp.where(arg >= 0, inverse, e * inverse)
        slopes.append((resist - goal) * (e * inverse * inverse) * (4.0 * scale))
    back = dot(tab["inter_rows_t"][...], stacked3(jnp.concatenate(slopes, axis=1)))
    back = jnp.concatenate([back[:, :TILE], back[:, TILE:]], axis=0)
    weight = dot3(back, tab["inter_cols_t"])
    pulled = []
    for j in range(TILES):
        at = j // (TILES // CONDS) * GRID
        w = weight[at : at + GRID]
        pulled.append(field[GRID * j : GRID * (j + 1)] * jnp.concatenate([w, w], axis=1))
    pulled = dot3(jnp.concatenate(pulled, axis=0), tab["field_cols_t"])
    pulled = jnp.concatenate(
        [
            jnp.concatenate([pulled[GRID * j : GRID * (j + 1), TILE * p : TILE * (p + 1)] for j in range(TILES)], axis=1)
            for p in range(2)
        ],
        axis=0,
    )
    pulled = dot(tab["field_rows_t"][...], stacked3(pulled))
    d_re = d_im = None
    for j in range(TILES):
        k_re, k_im = kk[0, j], kk[1, j]
        p_re = pulled[:BAND, TILE * j : TILE * (j + 1)]
        p_im = pulled[BAND:, TILE * j : TILE * (j + 1)]
        re, im = k_re * p_re + k_im * p_im, k_re * p_im - k_im * p_re
        d_re, d_im = (re, im) if d_re is None else (d_re + re, d_im + im)
    last = dot3(jnp.concatenate([d_re, d_im], axis=1), tab["last_cols"])
    swap[0, :BAND] = last[:, :TILE]
    swap[0, BAND:] = last[:, TILE:]
    copy = pltpu.make_async_remote_copy(
        src_ref=swap.at[0],
        dst_ref=swap.at[1],
        send_sem=send_sem.at[len(OFFSETS)],
        recv_sem=recv_sem.at[len(OFFSETS)],
        device_id=(row, col, 1 - core),
        device_id_type=MESH,
    )
    copy.start()
    for i in range(len(OFFSETS)):

        @pl.when(there[len(OFFSETS) - 1 - i])
        def _(i=i):
            sends[i].wait_send()

    copy.wait()
    out_ref[...] = swap[0] + swap[1]


def last_kernel(table_ref, sums_ref, out_ref):
    out_ref[...] = dot(table_ref[...], stacked3(sums_ref[...]))


def shards(mask, target, cond_index, kernels, dose):
    any_spec = pl.BlockSpec(memory_space=pl.ANY)
    vmem = pl.BlockSpec(memory_space=pltpu.VMEM)
    tables = [jnp.asarray(TABLES[name]) for name in NAMES]
    by_kernel = jnp.transpose(kernels, (0, 2, 1, 3))
    sums = pl.pallas_call(
        main_kernel,
        out_shape=jax.ShapeDtypeStruct((2 * BAND, TILE), F32),
        in_specs=[any_spec] * (5 + len(tables)),
        out_specs=vmem,
        scratch_shapes=[pltpu.VMEM(x.shape, x.dtype) for x in tables]
        + [
            pltpu.VMEM(mask.shape, F32),
            pltpu.VMEM(target.shape, jnp.int32),
            pltpu.VMEM(by_kernel.shape, F32),
            pltpu.SMEM(cond_index.shape, jnp.int32),
            pltpu.SMEM(dose.shape, F32),
            pltpu.VMEM((2, TILES, BAND, TILE), F32),
            pltpu.VMEM((len(OFFSETS), PACK, TILE), F32),
            pltpu.VMEM((len(OFFSETS), PACK, TILE), F32),
            pltpu.VMEM((2, 2 * BAND, TILE), F32),
            pltpu.SemaphoreType.DMA((len(tables) + 5,)),
            pltpu.SemaphoreType.DMA((len(OFFSETS) + 1,)),
            pltpu.SemaphoreType.DMA((len(OFFSETS) + 1,)),
        ],
        compiler_params=pltpu.CompilerParams(
            collective_id=0, has_side_effects=True, vmem_limit_bytes=63 * 1024 * 1024
        ),
        name="spectra_and_gradient",
    )(mask, target, by_kernel, cond_index, dose, *tables)
    return pl.pallas_call(
        last_kernel,
        out_shape=jax.ShapeDtypeStruct(mask.shape, F32),
        in_specs=[vmem, vmem],
        out_specs=vmem,
        name="to_pixels",
    )(jnp.asarray(TABLES["last_rows"]), sums)


def solution(mesh):
    in_specs = (P("row", "col"), P("row", "col"), P("cond"), P(), P())
    out_specs = P("row", "col")
    return jax.shard_map(shards, mesh=mesh, in_specs=in_specs, out_specs=out_specs, check_vma=False)
```

```python
import functools
import math

import jax
import jax.numpy as jnp
import ml_dtypes
import numpy as np
from jax import lax
from jax.experimental import pallas as pl
from jax.experimental.pallas import tpu as pltpu
from jax.sharding import PartitionSpec as P

MESH = pl.DeviceIdType.MESH
BF = jnp.bfloat16
F32 = jnp.float32

TILE = 128
MARGIN = 128
WINDOW = TILE + 2 * MARGIN
BAND = 24
KERNELS = 12
HALF = BAND // 2
REAL = 2 * HALF + 1
PACK = 5
GRID = 48
GROUP = 4
CONDS = 2
TILES = CONDS * KERNELS // GROUP
STEEP = 4.0
THRESH = 0.6
OFFSETS = [(-1, -1), (-1, 1), (0, -1), (-1, 0), (1, 0), (0, 1), (1, -1), (1, 1)]
ORDER = [(0, 6, 2), (1, 7, 5), (3, 4)]
FREQ = np.arange(BAND) - HALF
UNIT = 2.0 * math.pi / WINDOW


def parts(table):
    high = table.astype(ml_dtypes.bfloat16)
    low = (table - high.astype(np.float64)).astype(ml_dtypes.bfloat16)
    return high, low


def left3(table):
    high, low = parts(table)
    return np.concatenate([high, high, low], axis=1)


def pair(table):
    return np.stack(parts(table))


def real_basis(positions):
    order = np.arange(HALF + 1)[:, None] * positions[None, :] % WINDOW * UNIT
    return np.concatenate([np.cos(order), np.sin(order)[1:]], axis=0)


def make_tables():
    t = {}
    pixels = np.arange(TILE)
    rows = np.zeros((3, PACK, 8, TILE))
    cols = np.zeros((3, TILE, TILE))
    for d in range(3):
        basis = real_basis(pixels + TILE * (d - 1))
        rows[d, :, :PACK] = basis.reshape(PACK, PACK, TILE)
        for j in range(PACK):
            cols[d, :, REAL * j : REAL * (j + 1)] = basis.T / WINDOW
    t["dft_rows"] = left3(rows.reshape(3 * PACK * 8, TILE))
    t["dft_cols"] = pair(cols.transpose(1, 0, 2).reshape(TILE, 3 * TILE))

    pick = np.zeros((PACK, BAND, 2 * TILE), np.float32)
    spread = np.zeros((2, TILE, 2, GROUP, 32))
    for row, f in enumerate(FREQ):
        a = abs(f)
        j, i = divmod(a, PACK)
        pick[i, row, REAL * j : REAL * (j + 1)] = 1.0
        if f:
            j, i = divmod(HALF + a, PACK)
            pick[i, row, TILE + REAL * j : TILE + REAL * (j + 1)] = np.sign(f)
    for j in range(PACK):
        for col, g in enumerate(FREQ):
            cos_at = REAL * j + abs(g)
            spread[0, cos_at, 0, :, col] = 1.0
            spread[1, cos_at, 1, :, col] = -1.0
            if g:
                sin_at = REAL * j + HALF + abs(g)
                spread[1, sin_at, 0, :, col] = -np.sign(g)
                spread[0, sin_at, 1, :, col] = -np.sign(g)
    t["pick"] = pick
    t["spread"] = spread.reshape(2 * TILE, 2 * TILE).astype(ml_dtypes.bfloat16)

    rows_of = np.zeros((BAND, BAND * BAND), np.float32)
    fold = np.zeros((BAND * BAND, GROUP, 32))
    for l in range(BAND * BAND):
        rows_of[l // BAND, l] = 1.0
        fold[l, :, l % BAND] = 1.0
    t["rows_of"] = rows_of
    t["fold"] = fold.reshape(BAND * BAND, TILE).astype(ml_dtypes.bfloat16)

    angle = FREQ[:, None] * np.arange(GRID)[None, :] % GRID * (2.0 * math.pi / GRID)
    c, s = np.cos(angle), np.sin(angle)
    field_rows = np.block([[c.T, -s.T], [s.T, c.T]])
    t["field_rows"] = left3(field_rows)
    t["field_rows_t"] = left3(field_rows.T)
    field_cols = np.zeros((2, GROUP, 32, 2, GROUP, 64))
    for k in range(GROUP):
        field_cols[0, k, :BAND, 0, k, :GRID] = c
        field_cols[1, k, :BAND, 0, k, :GRID] = -s
        field_cols[0, k, :BAND, 1, k, :GRID] = s
        field_cols[1, k, :BAND, 1, k, :GRID] = c
    field_cols = field_cols.reshape(2 * TILE, 4 * TILE)
    t["field_cols"] = pair(field_cols)
    t["field_cols_t"] = pair(field_cols.T.copy())

    step = WINDOW // GRID
    gap = pixels[:, None] - step * np.arange(GRID)[None, :]
    orders = np.arange(1, GRID // 2)
    inter = (1.0 + 2.0 * np.cos(orders * gap[:, :, None] * UNIT).sum(-1)) / GRID
    inter_wide = np.zeros((TILE, GROUP, 64))
    inter_wide[:, :, :GRID] = inter[:, None, :]
    inter_wide = inter_wide.reshape(TILE, 2 * TILE)
    t["inter_rows"] = left3(inter)
    t["inter_rows_t"] = left3(inter.T)
    t["inter_cols"] = pair(inter_wide.T.copy())
    t["inter_cols_t"] = pair(inter_wide)

    turn = FREQ[:, None] * pixels[None, :] % WINDOW * UNIT
    c, s = np.cos(turn), np.sin(turn)
    last_cols = np.zeros((2, GROUP, 32, 2, TILE))
    last_cols[0, :, :BAND, 0] = c / WINDOW
    last_cols[1, :, :BAND, 0] = -s / WINDOW
    last_cols[0, :, :BAND, 1] = -s / WINDOW
    last_cols[1, :, :BAND, 1] = -c / WINDOW
    t["last_cols"] = pair(last_cols.reshape(2 * TILE, 2 * TILE))
    t["last_rows"] = left3(np.concatenate([c, s], axis=0).T)
    return t


TABLES = make_tables()
NAMES = [
    "dft_rows", "dft_cols", "rows_of", "fold", "pick", "spread", "field_rows", "field_cols",
    "inter_cols", "inter_rows", "inter_rows_t", "inter_cols_t", "field_cols_t", "field_rows_t", "last_cols",
    "last_rows",
]

LOADS = ("kernels", "cond", "dose", "rows_of", "fold")


def split(x):
    high = x.astype(BF)
    return high, (x - high.astype(F32)).astype(BF)


def dot(a, b):
    return jnp.dot(a, b, preferred_element_type=F32)


def dot3(x, table):
    high, low = split(x)
    return dot(high, table[0]) + dot(low, table[0]) + dot(high, table[1])


def stacked3(x):
    high, low = split(x)
    return jnp.concatenate([high, low, high], axis=0)


def main_kernel(*refs):
    n = len(NAMES)
    mask_hbm, target_hbm, kernels_hbm, cond_hbm, dose_hbm = refs[:5]
    tables_hbm = refs[5 : 5 + n]
    table_ref, out_ref = refs[5 + n : 7 + n]
    scratch = refs[7 + n :]
    tab = dict(zip(NAMES, list(scratch[: n - 1]) + [table_ref]))
    mask, target, kernels, cond_ref, dose_ref, kk, sent, held, swap, load_sem, send_sem, recv_sem = scratch[n - 1 :]

    row, col, core = (lax.axis_index(a) for a in ("row", "col", "cond"))
    n_row, n_col = lax.axis_size("row"), lax.axis_size("col")

    copies = {}
    first = [("mask", mask_hbm, mask)] + [(m, s, tab[m]) for m, s in zip(NAMES[:2], tables_hbm[:2])]
    later = (
        [("kernels", kernels_hbm, kernels), ("cond", cond_hbm, cond_ref), ("dose", dose_hbm, dose_ref)]
        + [(m, s, tab[m]) for m, s in zip(NAMES[2:], tables_hbm[2:])]
        + [("target", target_hbm, target)]
    )
    for i, (name, src, dst) in enumerate(first + later):
        copies[name] = pltpu.make_async_copy(src, dst, load_sem.at[i])
    for name, _, _ in first:
        copies[name].start()

    held[...] = jnp.zeros_like(held)
    barrier = pltpu.get_barrier_semaphore()
    pl.semaphore_signal(barrier, inc=1, device_id=(row, col, 1 - core), device_id_type=MESH)
    there = []
    count = jnp.int32(1)
    for dr, dc in OFFSETS:
        ok = (row + dr >= 0) & (row + dr < n_row) & (col + dc >= 0) & (col + dc < n_col)
        sender = 0 if dc == 0 else 1
        there.append(ok)
        count = count + jnp.where(ok & (core == sender), 2, 0)

        @pl.when(ok)
        def _():
            pl.semaphore_signal(barrier, inc=1, device_id=(row + dr, col + dc, sender), device_id_type=MESH)

    for name in ("mask", "dft_rows", "dft_cols"):
        copies[name].wait()
    lanes = lax.broadcasted_iota(jnp.int32, (8, TILE), 1)
    partial = dot(tab["dft_rows"][...], stacked3(mask[...]))
    partial = split(partial)

    def blocks_of(e):
        table = [tab["dft_cols"][p, :, TILE * e : TILE * (e + 1)] for p in range(2)]
        products = dot(partial[0], table[0]) + dot(partial[1], table[0]) + dot(partial[0], table[1])
        own = None
        for d in range(3):
            block = None
            for j in range(PACK):
                piece = products[8 * (PACK * d + j) : 8 * (PACK * d + j + 1)]
                block = piece if block is None else jnp.where(lanes < REAL * j, block, piece)
            if d == 1 and e == 1:
                own = block
            else:
                sent[OFFSETS.index((d - 1, e - 1))] = block[:PACK]
        return own

    sends = {}

    def send(order):
        for i in order:
            dr, dc = OFFSETS[i]
            for target in range(2):
                sends[i, target] = pltpu.make_async_remote_copy(
                    src_ref=sent.at[i],
                    dst_ref=held.at[i],
                    send_sem=send_sem.at[2 * i + target],
                    recv_sem=recv_sem.at[i],
                    device_id=(row - dr, col - dc, target),
                    device_id_type=MESH,
                )

                @pl.when(there[len(OFFSETS) - 1 - i] & (core == (0 if dc == 0 else 1)))
                def _():
                    sends[i, target].start()

    blocks_of(0)
    ahead = jnp.where(lax.rem(col, 2) == 0, TILES, 0)

    lane = lax.broadcasted_iota(jnp.int32, (BAND, TILE), 1) // 32

    def arrange(step, carry):
        c = step // 3
        group = step - 3 * c
        setting = cond_ref[c]
        for part in range(2):
            total = jnp.zeros((BAND, TILE), F32)
            for k in range(GROUP):
                line = kernels[setting, group * GROUP + k, part : part + 1, :]
                high, low = split(line * tab["rows_of"][...])
                folded = dot(high, tab["fold"][...]) + dot(low, tab["fold"][...])
                total = total + jnp.where(lane == k, folded, 0.0)
            kk[part, step] = total
        return carry

    @pl.when(ahead > 0)
    def _():
        for name, _, _ in later:
            copies[name].start()
        for name in LOADS:
            copies[name].wait()
        lax.fori_loop(0, TILES, arrange, 0)

    pl.semaphore_wait(barrier, count)
    send(ORDER[0])
    blocks_of(2)
    send(ORDER[1])
    own = blocks_of(1)
    send(ORDER[2])

    @pl.when(ahead == 0)
    def _():
        for name, _, _ in later:
            copies[name].start()
        for name in LOADS:
            copies[name].wait()
        lax.fori_loop(0, TILES, arrange, 0)

    for name in NAMES[4:] + ["target"]:
        copies[name].wait()
    doses = [dose_ref[cond_ref[c]] for c in range(CONDS)]
    goal = target[...].astype(F32)

    for i in range(len(OFFSETS)):

        @pl.when(there[i])
        def _(i=i):
            sends[i, 0].wait_recv()

    z = own[:PACK]
    for i in range(len(OFFSETS)):
        z = z + held[i]
    chosen = None
    for i in range(PACK):
        line = jnp.concatenate([z[i : i + 1], z[i : i + 1]], axis=1)
        piece = line * tab["pick"][i]
        chosen = piece if chosen is None else chosen + piece
    high, low = split(chosen)
    spectrum = dot(high, tab["spread"][...]) + dot(low, tab["spread"][...])
    s_re, s_im = spectrum[:, :TILE], spectrum[:, TILE:]
    product = []
    for j in range(TILES):
        k_re, k_im = kk[0, j], kk[1, j]
        product.append(jnp.concatenate([k_re * s_re - k_im * s_im, k_re * s_im + k_im * s_re], axis=0))
    along = dot(tab["field_rows"][...], stacked3(jnp.concatenate(product, axis=1)))
    along = jnp.concatenate(
        [
            jnp.concatenate([along[:GRID, TILE * j : TILE * (j + 1)], along[GRID:, TILE * j : TILE * (j + 1)]], axis=1)
            for j in range(TILES)
        ],
        axis=0,
    )
    field = dot3(along, tab["field_cols"])
    square = field * field
    square = square[:, : 2 * TILE] + square[:, 2 * TILE :]
    samples = []
    for c in range(CONDS):
        at = c * (TILES // CONDS) * GRID
        samples.append(square[at : at + GRID] + square[at + GRID : at + 2 * GRID] + square[at + 2 * GRID : at + 3 * GRID])
    inten = dot3(jnp.concatenate(samples, axis=0), tab["inter_cols"])
    inten = jnp.concatenate([inten[:GRID], inten[GRID:]], axis=1)
    inten = dot(tab["inter_rows"][...], stacked3(inten))
    slopes = []
    for c in range(CONDS):
        scale = doses[c] * (STEEP / (KERNELS * BAND * BAND))
        arg = scale * inten[:, TILE * c : TILE * (c + 1)] - STEEP * THRESH
        e = jnp.exp(-jnp.abs(arg))
        inverse = 1.0 / (1.0 + e)
        resist = jnp.where(arg >= 0, inverse, e * inverse)
        slopes.append((resist - goal) * (e * inverse * inverse) * (4.0 * scale))
    back = dot(tab["inter_rows_t"][...], stacked3(jnp.concatenate(slopes, axis=1)))
    back = jnp.concatenate([back[:, :TILE], back[:, TILE:]], axis=0)
    weight = dot3(back, tab["inter_cols_t"])
    pulled = []
    for j in range(TILES):
        at = j // (TILES // CONDS) * GRID
        w = weight[at : at + GRID]
        pulled.append(field[GRID * j : GRID * (j + 1)] * jnp.concatenate([w, w], axis=1))
    pulled = dot3(jnp.concatenate(pulled, axis=0), tab["field_cols_t"])
    pulled = jnp.concatenate(
        [
            jnp.concatenate([pulled[GRID * j : GRID * (j + 1), TILE * p : TILE * (p + 1)] for j in range(TILES)], axis=1)
            for p in range(2)
        ],
        axis=0,
    )
    pulled = dot(tab["field_rows_t"][...], stacked3(pulled))
    d_re = d_im = None
    for j in range(TILES):
        k_re, k_im = kk[0, j], kk[1, j]
        p_re = pulled[:BAND, TILE * j : TILE * (j + 1)]
        p_im = pulled[BAND:, TILE * j : TILE * (j + 1)]
        re, im = k_re * p_re + k_im * p_im, k_re * p_im - k_im * p_re
        d_re, d_im = (re, im) if d_re is None else (d_re + re, d_im + im)
    last = dot3(jnp.concatenate([d_re, d_im], axis=1), tab["last_cols"])
    swap[0, :BAND] = last[:, :TILE]
    swap[0, BAND:] = last[:, TILE:]
    copy = pltpu.make_async_remote_copy(
        src_ref=swap.at[0],
        dst_ref=swap.at[1],
        send_sem=send_sem.at[2 * len(OFFSETS)],
        recv_sem=recv_sem.at[len(OFFSETS)],
        device_id=(row, col, 1 - core),
        device_id_type=MESH,
    )
    copy.start()
    for i, (dr, dc) in enumerate(OFFSETS):

        @pl.when(there[len(OFFSETS) - 1 - i] & (core == (0 if dc == 0 else 1)))
        def _(i=i):
            for target in range(2):
                sends[i, target].wait_send()

    copy.wait()
    out_ref[...] = stacked3(swap[0] + swap[1])


def last_kernel(table_ref, sums_ref, out_ref):
    out_ref[...] = dot(table_ref[...], sums_ref[...])


def shards(mask, target, cond_index, kernels, dose):
    any_spec = pl.BlockSpec(memory_space=pl.ANY)
    vmem = pl.BlockSpec(memory_space=pltpu.VMEM)
    tables = [jnp.asarray(TABLES[name]) for name in NAMES]
    by_kernel = jnp.transpose(kernels, (0, 2, 1, 3))
    handed = pl.pallas_call(
        main_kernel,
        out_shape=[pltpu.VMEM(tables[-1].shape, BF), pltpu.VMEM((6 * BAND, TILE), BF)],
        in_specs=[any_spec] * (5 + len(tables)),
        out_specs=[vmem, vmem],
        scratch_shapes=[pltpu.VMEM(x.shape, x.dtype) for x in tables[:-1]]
        + [
            pltpu.VMEM(mask.shape, F32),
            pltpu.VMEM(target.shape, jnp.int32),
            pltpu.VMEM(by_kernel.shape, F32),
            pltpu.SMEM(cond_index.shape, jnp.int32),
            pltpu.SMEM(dose.shape, F32),
            pltpu.VMEM((2, TILES, BAND, TILE), F32),
            pltpu.VMEM((len(OFFSETS), PACK, TILE), F32),
            pltpu.VMEM((len(OFFSETS), PACK, TILE), F32),
            pltpu.VMEM((2, 2 * BAND, TILE), F32),
            pltpu.SemaphoreType.DMA((len(tables) + 5,)),
            pltpu.SemaphoreType.DMA((2 * len(OFFSETS) + 1,)),
            pltpu.SemaphoreType.DMA((len(OFFSETS) + 1,)),
        ],
        compiler_params=pltpu.CompilerParams(
            collective_id=0, has_side_effects=True, vmem_limit_bytes=63 * 1024 * 1024
        ),
        name="spectra_and_gradient",
    )(mask, target, by_kernel, cond_index, dose, *tables)
    return pl.pallas_call(
        last_kernel,
        out_shape=jax.ShapeDtypeStruct(mask.shape, F32),
        in_specs=[vmem, vmem],
        out_specs=vmem,
        name="to_pixels",
    )(*[pltpu.with_memory_space_constraint(x, pltpu.VMEM) for x in handed])


def solution(mesh):
    in_specs = (P("row", "col"), P("row", "col"), P("cond"), P(), P())
    out_specs = P("row", "col")
    return jax.shard_map(shards, mesh=mesh, in_specs=in_specs, out_specs=out_specs, check_vma=False)
```

```python
import functools
import math

import jax
import jax.numpy as jnp
import ml_dtypes
import numpy as np
from jax import lax
from jax.experimental import pallas as pl
from jax.experimental.pallas import tpu as pltpu
from jax.sharding import PartitionSpec as P

MESH = pl.DeviceIdType.MESH
BF = jnp.bfloat16
F32 = jnp.float32

TILE = 128
MARGIN = 128
WINDOW = TILE + 2 * MARGIN
BAND = 24
KERNELS = 12
HALF = BAND // 2
REAL = 2 * HALF + 1
PACK = 5
GRID = 48
GROUP = 4
CONDS = 4
OWN = 2
PER_COND = KERNELS // GROUP
SLABS = 2 * OWN * PER_COND
STEEP = 4.0
THRESH = 0.6
OFFSETS = [(-1, -1), (-1, 1), (0, -1), (-1, 0), (1, 0), (0, 1), (1, -1), (1, 1)]
ORDER = [(0, 6, 2), (1, 7, 5), (3, 4)]
FREQ = np.arange(BAND) - HALF
UNIT = 2.0 * math.pi / WINDOW


def parts(table):
    high = table.astype(ml_dtypes.bfloat16)
    low = (table - high.astype(np.float64)).astype(ml_dtypes.bfloat16)
    return high, low


def left3(table):
    high, low = parts(table)
    return np.concatenate([high, high, low], axis=1)


def pair(table):
    return np.stack(parts(table))


def real_basis(positions):
    order = np.arange(HALF + 1)[:, None] * positions[None, :] % WINDOW * UNIT
    return np.concatenate([np.cos(order), np.sin(order)[1:]], axis=0)


def make_tables():
    t = {}
    pixels = np.arange(TILE)
    rows = np.zeros((3, PACK, 8, TILE))
    cols = np.zeros((3, TILE, TILE))
    for d in range(3):
        basis = real_basis(pixels + TILE * (d - 1))
        rows[d, :, :PACK] = basis.reshape(PACK, PACK, TILE)
        for j in range(PACK):
            cols[d, :, REAL * j : REAL * (j + 1)] = basis.T / WINDOW
    t["dft_rows"] = left3(rows.reshape(3 * PACK * 8, TILE))
    t["dft_cols"] = pair(cols.transpose(1, 0, 2).reshape(TILE, 3 * TILE))

    pick = np.zeros((PACK, BAND, 2 * TILE), np.float32)
    spread = np.zeros((2, TILE, 2, GROUP, 32))
    for row, f in enumerate(FREQ):
        a = abs(f)
        j, i = divmod(a, PACK)
        pick[i, row, REAL * j : REAL * (j + 1)] = 1.0
        if f:
            j, i = divmod(HALF + a, PACK)
            pick[i, row, TILE + REAL * j : TILE + REAL * (j + 1)] = np.sign(f)
    for j in range(PACK):
        for col, g in enumerate(FREQ):
            cos_at = REAL * j + abs(g)
            spread[0, cos_at, 0, :, col] = 1.0
            spread[1, cos_at, 1, :, col] = -1.0
            if g:
                sin_at = REAL * j + HALF + abs(g)
                spread[1, sin_at, 0, :, col] = -np.sign(g)
                spread[0, sin_at, 1, :, col] = -np.sign(g)
    t["pick"] = pick
    t["spread"] = spread.reshape(2 * TILE, 2 * TILE).astype(ml_dtypes.bfloat16)

    rows_of = np.zeros((BAND, BAND * BAND), np.float32)
    fold = np.zeros((BAND * BAND, GROUP, 32))
    for l in range(BAND * BAND):
        rows_of[l // BAND, l] = 1.0
        fold[l, :, l % BAND] = 1.0
    t["rows_of"] = rows_of
    t["fold"] = fold.reshape(BAND * BAND, TILE).astype(ml_dtypes.bfloat16)

    angle = FREQ[:, None] * np.arange(GRID)[None, :] % GRID * (2.0 * math.pi / GRID)
    c, s = np.cos(angle), np.sin(angle)
    field_rows = np.block([[c.T, -s.T], [s.T, c.T]])
    t["field_rows"] = left3(field_rows)
    t["field_rows_t"] = left3(field_rows.T)
    field_cols = np.zeros((2, GROUP, 32, 2, GROUP, 64))
    for k in range(GROUP):
        field_cols[0, k, :BAND, 0, k, :GRID] = c
        field_cols[1, k, :BAND, 0, k, :GRID] = -s
        field_cols[0, k, :BAND, 1, k, :GRID] = s
        field_cols[1, k, :BAND, 1, k, :GRID] = c
    field_cols = field_cols.reshape(2 * TILE, 4 * TILE)
    t["field_cols"] = pair(field_cols)
    t["field_cols_t"] = pair(field_cols.T.copy())

    step = WINDOW // GRID
    gap = pixels[:, None] - step * np.arange(GRID)[None, :]
    orders = np.arange(1, GRID // 2)
    inter = (1.0 + 2.0 * np.cos(orders * gap[:, :, None] * UNIT).sum(-1)) / GRID
    inter_wide = np.zeros((TILE, GROUP, 64))
    inter_wide[:, :, :GRID] = inter[:, None, :]
    inter_wide = inter_wide.reshape(TILE, 2 * TILE)
    t["inter_rows"] = left3(inter)
    t["inter_rows_t"] = left3(inter.T)
    t["inter_cols"] = pair(inter_wide.T.copy())
    t["inter_cols_t"] = pair(inter_wide)

    turn = FREQ[:, None] * pixels[None, :] % WINDOW * UNIT
    c, s = np.cos(turn), np.sin(turn)
    last_cols = np.zeros((2, GROUP, 32, 2, TILE))
    last_cols[0, :, :BAND, 0] = c / WINDOW
    last_cols[1, :, :BAND, 0] = -s / WINDOW
    last_cols[0, :, :BAND, 1] = -s / WINDOW
    last_cols[1, :, :BAND, 1] = -c / WINDOW
    t["last_cols"] = pair(last_cols.reshape(2 * TILE, 2 * TILE))
    t["last_rows"] = left3(np.concatenate([c, s], axis=0).T)
    return t


TABLES = make_tables()
NAMES = [
    "dft_rows", "dft_cols", "rows_of", "fold", "pick", "spread", "field_rows", "field_cols",
    "inter_cols", "inter_rows", "inter_rows_t", "inter_cols_t", "field_cols_t", "field_rows_t", "last_cols",
    "last_rows",
]

LOADS = ("kernels", "cond", "dose", "rows_of", "fold")


def split(x):
    high = x.astype(BF)
    return high, (x - high.astype(F32)).astype(BF)


def dot(a, b):
    return jnp.dot(a, b, preferred_element_type=F32)


def dot3(x, table):
    high, low = split(x)
    return dot(high, table[0]) + dot(low, table[0]) + dot(high, table[1])


def stacked3(x):
    high, low = split(x)
    return jnp.concatenate([high, low, high], axis=0)


def main_kernel(*refs):
    n = len(NAMES)
    mask_hbm, target_hbm, kernels_hbm, cond_hbm, dose_hbm = refs[:5]
    tables_hbm = refs[5 : 5 + n]
    table_ref, out_ref = refs[5 + n : 7 + n]
    scratch = refs[7 + n :]
    tab = dict(zip(NAMES, list(scratch[: n - 1]) + [table_ref]))
    mask, target, kernels, cond_ref, dose_ref, kk, sent, held, load_sem, send_sem, recv_sem = scratch[n - 1 :]

    row, col, core = (lax.axis_index(a) for a in ("row", "col", "cond"))
    n_row, n_col = lax.axis_size("row"), lax.axis_size("col")

    copies = {}
    first = [("mask", mask_hbm, mask)] + [(m, s, tab[m]) for m, s in zip(NAMES[:2], tables_hbm[:2])]
    later = (
        [("kernels", kernels_hbm, kernels), ("cond", cond_hbm, cond_ref), ("dose", dose_hbm, dose_ref)]
        + [(m, s, tab[m]) for m, s in zip(NAMES[2:], tables_hbm[2:])]
        + [("target", target_hbm, target)]
    )
    for i, (name, src, dst) in enumerate(first + later):
        copies[name] = pltpu.make_async_copy(src, dst, load_sem.at[i])
    for name, _, _ in first:
        copies[name].start()

    held[...] = jnp.zeros_like(held)
    even = lax.rem(col, 2) == 0

    def from_core(dr, dc, at_row, at_col, at_core):
        return jnp.where((at_row == 0) & (at_col == 0) & (at_core == 0), 0, 1) if dc else 0

    barrier = pltpu.get_barrier_semaphore()
    pl.semaphore_signal(barrier, inc=1, device_id=(row, col, 1 - core), device_id_type=MESH)
    there = []
    count = jnp.int32(1)
    for dr, dc in OFFSETS:
        ok = (row + dr >= 0) & (row + dr < n_row) & (col + dc >= 0) & (col + dc < n_col)
        there.append(ok)
        for to in range(2):
            count = count + jnp.where(ok & (core == from_core(dr, dc, row + dr, col + dc, to)), 1, 0)
        sender = from_core(dr, dc, row, col, core)

        @pl.when(ok)
        def _():
            pl.semaphore_signal(barrier, inc=1, device_id=(row + dr, col + dc, sender), device_id_type=MESH)

    def sending(i, to):
        dr, dc = OFFSETS[i]
        return there[len(OFFSETS) - 1 - i] & (core == from_core(dr, dc, row - dr, col - dc, to))

    for name in ("mask", "dft_rows", "dft_cols"):
        copies[name].wait()
    lanes = lax.broadcasted_iota(jnp.int32, (8, TILE), 1)
    partial = dot(tab["dft_rows"][...], stacked3(mask[...]))
    partial = split(partial)

    def blocks_of(e):
        table = [tab["dft_cols"][p, :, TILE * e : TILE * (e + 1)] for p in range(2)]
        products = dot(partial[0], table[0]) + dot(partial[1], table[0]) + dot(partial[0], table[1])
        own = None
        for d in range(3):
            block = None
            for j in range(PACK):
                piece = products[8 * (PACK * d + j) : 8 * (PACK * d + j + 1)]
                block = piece if block is None else jnp.where(lanes < REAL * j, block, piece)
            if d == 1 and e == 1:
                own = block
            else:
                sent[OFFSETS.index((d - 1, e - 1))] = block[:PACK]
        return own

    sends = {}

    def send(order):
        for i in order:
            dr, dc = OFFSETS[i]
            for to in range(2):
                sends[i, to] = pltpu.make_async_remote_copy(
                    src_ref=sent.at[i],
                    dst_ref=held.at[i],
                    send_sem=send_sem.at[2 * i + to],
                    recv_sem=recv_sem.at[i],
                    device_id=(row - dr, col - dc, to),
                    device_id_type=MESH,
                )

                @pl.when(sending(i, to))
                def _():
                    sends[i, to].start()

    blocks_of(0)
    lane = lax.broadcasted_iota(jnp.int32, (BAND, TILE), 1) // 32

    def arrange(step, carry):
        c = step // PER_COND
        group = step - PER_COND * c
        setting = cond_ref[c]
        for part in range(2):
            total = jnp.zeros((BAND, TILE), F32)
            for k in range(GROUP):
                line = kernels[setting, group * GROUP + k, part : part + 1, :]
                high, low = split(line * tab["rows_of"][...])
                folded = dot(high, tab["fold"][...]) + dot(low, tab["fold"][...])
                total = total + jnp.where(lane == k, folded, 0.0)
            kk[0, OWN * PER_COND * part + step] = total
        return carry

    def arrange_all():
        for name, _, _ in later:
            copies[name].start()
        for name in LOADS:
            copies[name].wait()
        for c in range(OWN):
            kk[0, SLABS, c : c + 1] = jnp.full((1, TILE), dose_ref[cond_ref[c]], F32)
        lax.fori_loop(0, OWN * PER_COND, arrange, 0)

    pl.when(even)(arrange_all)

    pl.semaphore_wait(barrier, count)
    send(ORDER[0])
    blocks_of(2)
    send(ORDER[1])
    own = blocks_of(1)
    send(ORDER[2])

    pl.when(jnp.logical_not(even))(arrange_all)
    share = pltpu.make_async_remote_copy(
        src_ref=kk.at[0],
        dst_ref=kk.at[1],
        send_sem=send_sem.at[2 * len(OFFSETS)],
        recv_sem=recv_sem.at[len(OFFSETS)],
        device_id=(row, col, 1 - core),
        device_id_type=MESH,
    )
    share.start()

    for name in NAMES[4:] + ["target"]:
        copies[name].wait()
    share.wait_recv()
    goal = target[...].astype(F32)

    for i in range(len(OFFSETS)):

        @pl.when(there[i])
        def _(i=i):
            sends[i, 0].wait_recv()

    z = own[:PACK]
    for i in range(len(OFFSETS)):
        z = z + held[i]
    chosen = None
    for i in range(PACK):
        line = jnp.concatenate([z[i : i + 1], z[i : i + 1]], axis=1)
        piece = line * tab["pick"][i]
        chosen = piece if chosen is None else chosen + piece
    high, low = split(chosen)
    spectrum = dot(high, tab["spread"][...]) + dot(low, tab["spread"][...])
    s_re, s_im = spectrum[:, :TILE], spectrum[:, TILE:]

    def kernel_tile(j):
        who, at = divmod(j, OWN * PER_COND)
        return kk[who, at], kk[who, OWN * PER_COND + at]

    product = []
    for j in range(CONDS * PER_COND):
        k_re, k_im = kernel_tile(j)
        product.append(jnp.concatenate([k_re * s_re - k_im * s_im, k_re * s_im + k_im * s_re], axis=0))
    along = dot(tab["field_rows"][...], stacked3(jnp.concatenate(product, axis=1)))
    along = jnp.concatenate(
        [
            jnp.concatenate([along[:GRID, TILE * j : TILE * (j + 1)], along[GRID:, TILE * j : TILE * (j + 1)]], axis=1)
            for j in range(CONDS * PER_COND)
        ],
        axis=0,
    )
    field = dot3(along, tab["field_cols"])
    square = field * field
    square = square[:, : 2 * TILE] + square[:, 2 * TILE :]
    samples = []
    for c in range(CONDS):
        at = c * PER_COND * GRID
        samples.append(square[at : at + GRID] + square[at + GRID : at + 2 * GRID] + square[at + 2 * GRID : at + 3 * GRID])
    inten = dot3(jnp.concatenate(samples, axis=0), tab["inter_cols"])
    inten = jnp.concatenate([inten[GRID * c : GRID * (c + 1)] for c in range(CONDS)], axis=1)
    inten = dot(tab["inter_rows"][...], stacked3(inten))
    slopes = []
    for c in range(CONDS):
        scale = kk[c // OWN, SLABS, c % OWN : c % OWN + 1] * (STEEP / (KERNELS * BAND * BAND))
        arg = scale * inten[:, TILE * c : TILE * (c + 1)] - STEEP * THRESH
        e = jnp.exp(-jnp.abs(arg))
        inverse = 1.0 / (1.0 + e)
        resist = jnp.where(arg >= 0, inverse, e * inverse)
        slopes.append((resist - goal) * (e * inverse * inverse) * (4.0 * scale))
    back = dot(tab["inter_rows_t"][...], stacked3(jnp.concatenate(slopes, axis=1)))
    back = jnp.concatenate([back[:, TILE * c : TILE * (c + 1)] for c in range(CONDS)], axis=0)
    weight = dot3(back, tab["inter_cols_t"])
    pulled = []
    for j in range(CONDS * PER_COND):
        at = j // PER_COND * GRID
        w = weight[at : at + GRID]
        pulled.append(field[GRID * j : GRID * (j + 1)] * jnp.concatenate([w, w], axis=1))
    pulled = dot3(jnp.concatenate(pulled, axis=0), tab["field_cols_t"])
    pulled = jnp.concatenate(
        [
            jnp.concatenate([pulled[GRID * j : GRID * (j + 1), TILE * p : TILE * (p + 1)] for j in range(CONDS * PER_COND)], axis=1)
            for p in range(2)
        ],
        axis=0,
    )
    pulled = dot(tab["field_rows_t"][...], stacked3(pulled))
    d_re = d_im = None
    for j in range(CONDS * PER_COND):
        k_re, k_im = kernel_tile(j)
        p_re = pulled[:BAND, TILE * j : TILE * (j + 1)]
        p_im = pulled[BAND:, TILE * j : TILE * (j + 1)]
        re, im = k_re * p_re + k_im * p_im, k_re * p_im - k_im * p_re
        d_re, d_im = (re, im) if d_re is None else (d_re + re, d_im + im)
    last = dot3(jnp.concatenate([d_re, d_im], axis=1), tab["last_cols"])
    out_ref[...] = stacked3(jnp.concatenate([last[:, :TILE], last[:, TILE:]], axis=0))
    share.wait_send()
    for i in range(len(OFFSETS)):
        for to in range(2):

            @pl.when(sending(i, to))
            def _(i=i, to=to):
                sends[i, to].wait_send()


def last_kernel(table_ref, sums_ref, out_ref):
    out_ref[...] = dot(table_ref[...], sums_ref[...])


def shards(mask, target, cond_index, kernels, dose):
    any_spec = pl.BlockSpec(memory_space=pl.ANY)
    vmem = pl.BlockSpec(memory_space=pltpu.VMEM)
    tables = [jnp.asarray(TABLES[name]) for name in NAMES]
    by_kernel = jnp.transpose(kernels, (0, 2, 1, 3))
    handed = pl.pallas_call(
        main_kernel,
        out_shape=[pltpu.VMEM(tables[-1].shape, BF), pltpu.VMEM((6 * BAND, TILE), BF)],
        in_specs=[any_spec] * (5 + len(tables)),
        out_specs=[vmem, vmem],
        scratch_shapes=[pltpu.VMEM(x.shape, x.dtype) for x in tables[:-1]]
        + [
            pltpu.VMEM(mask.shape, F32),
            pltpu.VMEM(target.shape, jnp.int32),
            pltpu.VMEM(by_kernel.shape, F32),
            pltpu.SMEM(cond_index.shape, jnp.int32),
            pltpu.SMEM(dose.shape, F32),
            pltpu.VMEM((2, SLABS + 1, BAND, TILE), F32),
            pltpu.VMEM((len(OFFSETS), PACK, TILE), F32),
            pltpu.VMEM((len(OFFSETS), PACK, TILE), F32),
            pltpu.SemaphoreType.DMA((len(tables) + 5,)),
            pltpu.SemaphoreType.DMA((2 * len(OFFSETS) + 1,)),
            pltpu.SemaphoreType.DMA((len(OFFSETS) + 1,)),
        ],
        compiler_params=pltpu.CompilerParams(
            collective_id=0, has_side_effects=True, vmem_limit_bytes=63 * 1024 * 1024
        ),
        name="spectra_and_gradient",
    )(mask, target, by_kernel, cond_index, dose, *tables)
    return pl.pallas_call(
        last_kernel,
        out_shape=jax.ShapeDtypeStruct(mask.shape, F32),
        in_specs=[vmem, vmem],
        out_specs=vmem,
        name="to_pixels",
    )(*[pltpu.with_memory_space_constraint(x, pltpu.VMEM) for x in handed])


def solution(mesh):
    in_specs = (P("row", "col"), P("row", "col"), P("cond"), P(), P())
    out_specs = P("row", "col")
    return jax.shard_map(shards, mesh=mesh, in_specs=in_specs, out_specs=out_specs, check_vma=False)
```

```python
import functools
import math

import jax
import jax.numpy as jnp
import ml_dtypes
import numpy as np
from jax import lax
from jax.experimental import pallas as pl
from jax.experimental.pallas import tpu as pltpu
from jax.sharding import PartitionSpec as P

MESH = pl.DeviceIdType.MESH
BF = jnp.bfloat16
F32 = jnp.float32

TILE = 128
MARGIN = 128
WINDOW = TILE + 2 * MARGIN
BAND = 24
KERNELS = 12
HALF = BAND // 2
REAL = 2 * HALF + 1
PACK = 5
GRID = 48
GROUP = 4
CONDS = 4
OWN = 2
PER_COND = KERNELS // GROUP
SLABS = 2 * OWN * PER_COND
STEEP = 4.0
THRESH = 0.6
OFFSETS = [(-1, -1), (-1, 1), (0, -1), (-1, 0), (1, 0), (0, 1), (1, -1), (1, 1)]
ORDER = [(0, 6, 2), (1, 7, 5), (3, 4)]
FREQ = np.arange(BAND) - HALF
UNIT = 2.0 * math.pi / WINDOW


def parts(table):
    high = table.astype(ml_dtypes.bfloat16)
    low = (table - high.astype(np.float64)).astype(ml_dtypes.bfloat16)
    return high, low


def left3(table):
    high, low = parts(table)
    return np.concatenate([high, high, low], axis=1)


def pair(table):
    return np.stack(parts(table))


def real_basis(positions):
    order = np.arange(HALF + 1)[:, None] * positions[None, :] % WINDOW * UNIT
    return np.concatenate([np.cos(order), np.sin(order)[1:]], axis=0)


def make_tables():
    t = {}
    pixels = np.arange(TILE)
    rows = np.zeros((3, PACK, 8, TILE))
    cols = np.zeros((3, TILE, TILE))
    for d in range(3):
        basis = real_basis(pixels + TILE * (d - 1))
        rows[d, :, :PACK] = basis.reshape(PACK, PACK, TILE)
        for j in range(PACK):
            cols[d, :, REAL * j : REAL * (j + 1)] = basis.T / WINDOW
    t["dft_rows"] = left3(rows.reshape(3 * PACK * 8, TILE))
    t["dft_cols"] = pair(cols.transpose(1, 0, 2).reshape(TILE, 3 * TILE))

    pick = np.zeros((PACK, BAND, 2 * TILE), np.float32)
    spread = np.zeros((2, TILE, 2, GROUP, 32))
    for row, f in enumerate(FREQ):
        a = abs(f)
        j, i = divmod(a, PACK)
        pick[i, row, REAL * j : REAL * (j + 1)] = 1.0
        if f:
            j, i = divmod(HALF + a, PACK)
            pick[i, row, TILE + REAL * j : TILE + REAL * (j + 1)] = np.sign(f)
    for j in range(PACK):
        for col, g in enumerate(FREQ):
            cos_at = REAL * j + abs(g)
            spread[0, cos_at, 0, :, col] = 1.0
            spread[1, cos_at, 1, :, col] = -1.0
            if g:
                sin_at = REAL * j + HALF + abs(g)
                spread[1, sin_at, 0, :, col] = -np.sign(g)
                spread[0, sin_at, 1, :, col] = -np.sign(g)
    t["pick"] = pick
    t["spread"] = spread.reshape(2 * TILE, 2 * TILE).astype(ml_dtypes.bfloat16)

    rows_of = np.zeros((BAND, BAND * BAND), np.float32)
    fold = np.zeros((BAND * BAND, GROUP, 32))
    for l in range(BAND * BAND):
        rows_of[l // BAND, l] = 1.0
        fold[l, :, l % BAND] = 1.0
    t["rows_of"] = rows_of
    t["fold"] = fold.reshape(BAND * BAND, TILE).astype(ml_dtypes.bfloat16)

    angle = FREQ[:, None] * np.arange(GRID)[None, :] % GRID * (2.0 * math.pi / GRID)
    c, s = np.cos(angle), np.sin(angle)
    field_rows = np.block([[c.T, -s.T], [s.T, c.T]])
    t["field_rows"] = left3(field_rows)
    t["field_rows_t"] = left3(field_rows.T)
    field_cols = np.zeros((2, GROUP, 32, 2, GROUP, 64))
    for k in range(GROUP):
        field_cols[0, k, :BAND, 0, k, :GRID] = c
        field_cols[1, k, :BAND, 0, k, :GRID] = -s
        field_cols[0, k, :BAND, 1, k, :GRID] = s
        field_cols[1, k, :BAND, 1, k, :GRID] = c
    field_cols = field_cols.reshape(2 * TILE, 4 * TILE)
    t["field_cols"] = pair(field_cols)
    t["field_cols_t"] = pair(field_cols.T.copy())

    step = WINDOW // GRID
    gap = pixels[:, None] - step * np.arange(GRID)[None, :]
    orders = np.arange(1, GRID // 2)
    inter = (1.0 + 2.0 * np.cos(orders * gap[:, :, None] * UNIT).sum(-1)) / GRID
    inter_wide = np.zeros((TILE, GROUP, 64))
    inter_wide[:, :, :GRID] = inter[:, None, :]
    inter_wide = inter_wide.reshape(TILE, 2 * TILE)
    t["inter_rows"] = left3(inter)
    t["inter_rows_t"] = left3(inter.T)
    t["inter_cols"] = pair(inter_wide.T.copy())
    t["inter_cols_t"] = pair(inter_wide)

    turn = FREQ[:, None] * pixels[None, :] % WINDOW * UNIT
    c, s = np.cos(turn), np.sin(turn)
    last_cols = np.zeros((2, GROUP, 32, 2, TILE))
    last_cols[0, :, :BAND, 0] = c / WINDOW
    last_cols[1, :, :BAND, 0] = -s / WINDOW
    last_cols[0, :, :BAND, 1] = -s / WINDOW
    last_cols[1, :, :BAND, 1] = -c / WINDOW
    t["last_cols"] = pair(last_cols.reshape(2 * TILE, 2 * TILE))
    t["last_rows"] = left3(np.concatenate([c, s], axis=0).T)
    return t


TABLES = make_tables()
NAMES = [
    "dft_rows", "dft_cols", "rows_of", "fold", "pick", "spread", "field_rows", "field_cols",
    "inter_cols", "inter_rows", "inter_rows_t", "inter_cols_t", "field_cols_t", "field_rows_t", "last_cols",
    "last_rows",
]

LOADS = ("kernels", "cond", "dose", "rows_of", "fold")


def split(x):
    high = x.astype(BF)
    return high, (x - high.astype(F32)).astype(BF)


def dot(a, b):
    return jnp.dot(a, b, preferred_element_type=F32)


def dot3(x, table):
    high, low = split(x)
    return dot(high, table[0]) + dot(low, table[0]) + dot(high, table[1])


def dot3_in(pieces, x, table):
    rows = x.shape[0] // pieces
    return jnp.concatenate([dot3(x[rows * i : rows * (i + 1)], table) for i in range(pieces)], axis=0)


def stacked3(x):
    high, low = split(x)
    return jnp.concatenate([high, low, high], axis=0)


def main_kernel(*refs):
    n = len(NAMES)
    mask_hbm, target_hbm, kernels_hbm, cond_hbm, dose_hbm = refs[:5]
    tables_hbm = refs[5 : 5 + n]
    table_ref, out_ref = refs[5 + n : 7 + n]
    scratch = refs[7 + n :]
    tab = dict(zip(NAMES, list(scratch[: n - 1]) + [table_ref]))
    mask, target, kernels, cond_ref, dose_ref, kk, sent, held, load_sem, send_sem, recv_sem = scratch[n - 1 :]

    row, col, core = (lax.axis_index(a) for a in ("row", "col", "cond"))
    n_row, n_col = lax.axis_size("row"), lax.axis_size("col")

    copies = {}
    first = [("mask", mask_hbm, mask)] + [(m, s, tab[m]) for m, s in zip(NAMES[:2], tables_hbm[:2])]
    later = (
        [("kernels", kernels_hbm, kernels), ("cond", cond_hbm, cond_ref), ("dose", dose_hbm, dose_ref)]
        + [(m, s, tab[m]) for m, s in zip(NAMES[2:], tables_hbm[2:])]
        + [("target", target_hbm, target)]
    )
    for i, (name, src, dst) in enumerate(first + later):
        copies[name] = pltpu.make_async_copy(src, dst, load_sem.at[i])
    for name, _, _ in first:
        copies[name].start()

    held[...] = jnp.zeros_like(held)
    even = lax.rem(col, 2) == 0

    def from_core(dr, dc, at_row, at_col, at_core):
        return jnp.where((at_row == 0) & (at_col == 0) & (at_core == 0), 0, 1) if dc else 0

    barrier = pltpu.get_barrier_semaphore()
    pl.semaphore_signal(barrier, inc=1, device_id=(row, col, 1 - core), device_id_type=MESH)
    there = []
    count = jnp.int32(1)
    for dr, dc in OFFSETS:
        ok = (row + dr >= 0) & (row + dr < n_row) & (col + dc >= 0) & (col + dc < n_col)
        there.append(ok)
        for to in range(2):
            count = count + jnp.where(ok & (core == from_core(dr, dc, row + dr, col + dc, to)), 1, 0)
        sender = from_core(dr, dc, row, col, core)

        @pl.when(ok)
        def _():
            pl.semaphore_signal(barrier, inc=1, device_id=(row + dr, col + dc, sender), device_id_type=MESH)

    def sending(i, to):
        dr, dc = OFFSETS[i]
        return there[len(OFFSETS) - 1 - i] & (core == from_core(dr, dc, row - dr, col - dc, to))

    for name in ("mask", "dft_rows", "dft_cols"):
        copies[name].wait()
    lanes = lax.broadcasted_iota(jnp.int32, (8, TILE), 1)
    partial = dot(tab["dft_rows"][...], stacked3(mask[...]))
    partial = split(partial)

    def blocks_of(e):
        table = [tab["dft_cols"][p, :, TILE * e : TILE * (e + 1)] for p in range(2)]
        products = dot(partial[0], table[0]) + dot(partial[1], table[0]) + dot(partial[0], table[1])
        own = None
        for d in range(3):
            block = None
            for j in range(PACK):
                piece = products[8 * (PACK * d + j) : 8 * (PACK * d + j + 1)]
                block = piece if block is None else jnp.where(lanes < REAL * j, block, piece)
            if d == 1 and e == 1:
                own = block
            else:
                sent[OFFSETS.index((d - 1, e - 1))] = block[:PACK]
        return own

    sends = {}

    def send(order):
        for i in order:
            dr, dc = OFFSETS[i]
            for to in range(2):
                sends[i, to] = pltpu.make_async_remote_copy(
                    src_ref=sent.at[i],
                    dst_ref=held.at[i],
                    send_sem=send_sem.at[2 * i + to],
                    recv_sem=recv_sem.at[i],
                    device_id=(row - dr, col - dc, to),
                    device_id_type=MESH,
                )

                @pl.when(sending(i, to))
                def _():
                    sends[i, to].start()

    blocks_of(0)
    lane = lax.broadcasted_iota(jnp.int32, (BAND, TILE), 1) // 32

    def arrange(step, carry):
        c = step // PER_COND
        group = step - PER_COND * c
        setting = cond_ref[c]
        for part in range(2):
            total = jnp.zeros((BAND, TILE), F32)
            for k in range(GROUP):
                line = kernels[setting, group * GROUP + k, part : part + 1, :]
                high, low = split(line * tab["rows_of"][...])
                folded = dot(high, tab["fold"][...]) + dot(low, tab["fold"][...])
                total = total + jnp.where(lane == k, folded, 0.0)
            kk[0, OWN * PER_COND * part + step] = total
        return carry

    def arrange_all():
        for name, _, _ in later:
            copies[name].start()
        for name in LOADS:
            copies[name].wait()
        for c in range(OWN):
            kk[0, SLABS, c : c + 1] = jnp.full((1, TILE), dose_ref[cond_ref[c]], F32)
        lax.fori_loop(0, OWN * PER_COND, arrange, 0)

    pl.when(even)(arrange_all)

    pl.semaphore_wait(barrier, count)
    send(ORDER[0])
    blocks_of(2)
    send(ORDER[1])
    own = blocks_of(1)
    send(ORDER[2])

    pl.when(jnp.logical_not(even))(arrange_all)
    share = pltpu.make_async_remote_copy(
        src_ref=kk.at[0],
        dst_ref=kk.at[1],
        send_sem=send_sem.at[2 * len(OFFSETS)],
        recv_sem=recv_sem.at[len(OFFSETS)],
        device_id=(row, col, 1 - core),
        device_id_type=MESH,
    )
    share.start()

    for name in NAMES[4:] + ["target"]:
        copies[name].wait()
    share.wait_recv()
    goal = target[...].astype(F32)

    for i in range(len(OFFSETS)):

        @pl.when(there[i])
        def _(i=i):
            sends[i, 0].wait_recv()

    z = own[:PACK]
    for i in range(len(OFFSETS)):
        z = z + held[i]
    chosen = None
    for i in range(PACK):
        line = jnp.concatenate([z[i : i + 1], z[i : i + 1]], axis=1)
        piece = line * tab["pick"][i]
        chosen = piece if chosen is None else chosen + piece
    high, low = split(chosen)
    spectrum = dot(high, tab["spread"][...]) + dot(low, tab["spread"][...])
    s_re, s_im = spectrum[:, :TILE], spectrum[:, TILE:]

    def kernel_tile(j):
        who, at = divmod(j, OWN * PER_COND)
        return kk[who, at], kk[who, OWN * PER_COND + at]

    product = []
    for j in range(CONDS * PER_COND):
        k_re, k_im = kernel_tile(j)
        product.append(jnp.concatenate([k_re * s_re - k_im * s_im, k_re * s_im + k_im * s_re], axis=0))
    along = dot(tab["field_rows"][...], stacked3(jnp.concatenate(product, axis=1)))
    along = jnp.concatenate(
        [
            jnp.concatenate([along[:GRID, TILE * j : TILE * (j + 1)], along[GRID:, TILE * j : TILE * (j + 1)]], axis=1)
            for j in range(CONDS * PER_COND)
        ],
        axis=0,
    )
    field = dot3(along, tab["field_cols"])
    square = field * field
    square = square[:, : 2 * TILE] + square[:, 2 * TILE :]
    samples = []
    for c in range(CONDS):
        at = c * PER_COND * GRID
        samples.append(square[at : at + GRID] + square[at + GRID : at + 2 * GRID] + square[at + 2 * GRID : at + 3 * GRID])
    inten = dot3_in(2, jnp.concatenate(samples, axis=0), tab["inter_cols"])
    inten = jnp.concatenate([inten[GRID * c : GRID * (c + 1)] for c in range(CONDS)], axis=1)
    inten = dot(tab["inter_rows"][...], stacked3(inten))
    slopes = []
    for c in range(CONDS):
        scale = kk[c // OWN, SLABS, c % OWN : c % OWN + 1] * (STEEP / (KERNELS * BAND * BAND))
        arg = scale * inten[:, TILE * c : TILE * (c + 1)] - STEEP * THRESH
        e = jnp.exp(-jnp.abs(arg))
        inverse = 1.0 / (1.0 + e)
        resist = jnp.where(arg >= 0, inverse, e * inverse)
        slopes.append((resist - goal) * (e * inverse * inverse) * (4.0 * scale))
    back = dot(tab["inter_rows_t"][...], stacked3(jnp.concatenate(slopes, axis=1)))
    back = jnp.concatenate([back[:, TILE * c : TILE * (c + 1)] for c in range(CONDS)], axis=0)
    weight = dot3_in(2, back, tab["inter_cols_t"])
    pulled = []
    for j in range(CONDS * PER_COND):
        at = j // PER_COND * GRID
        w = weight[at : at + GRID]
        pulled.append(field[GRID * j : GRID * (j + 1)] * jnp.concatenate([w, w], axis=1))
    pulled = dot3_in(2, jnp.concatenate(pulled, axis=0), tab["field_cols_t"])
    pulled = jnp.concatenate(
        [
            jnp.concatenate([pulled[GRID * j : GRID * (j + 1), TILE * p : TILE * (p + 1)] for j in range(CONDS * PER_COND)], axis=1)
            for p in range(2)
        ],
        axis=0,
    )
    pulled = dot(tab["field_rows_t"][...], stacked3(pulled))
    d_re = d_im = None
    for j in range(CONDS * PER_COND):
        k_re, k_im = kernel_tile(j)
        p_re = pulled[:BAND, TILE * j : TILE * (j + 1)]
        p_im = pulled[BAND:, TILE * j : TILE * (j + 1)]
        re, im = k_re * p_re + k_im * p_im, k_re * p_im - k_im * p_re
        d_re, d_im = (re, im) if d_re is None else (d_re + re, d_im + im)
    last = dot3(jnp.concatenate([d_re, d_im], axis=1), tab["last_cols"])
    out_ref[...] = stacked3(jnp.concatenate([last[:, :TILE], last[:, TILE:]], axis=0))
    share.wait_send()
    for i in range(len(OFFSETS)):
        for to in range(2):

            @pl.when(sending(i, to))
            def _(i=i, to=to):
                sends[i, to].wait_send()


def last_kernel(table_ref, sums_ref, out_ref):
    out_ref[...] = dot(table_ref[...], sums_ref[...])


def shards(mask, target, cond_index, kernels, dose):
    any_spec = pl.BlockSpec(memory_space=pl.ANY)
    vmem = pl.BlockSpec(memory_space=pltpu.VMEM)
    tables = [jnp.asarray(TABLES[name]) for name in NAMES]
    by_kernel = jnp.transpose(kernels, (0, 2, 1, 3))
    handed = pl.pallas_call(
        main_kernel,
        out_shape=[pltpu.VMEM(tables[-1].shape, BF), pltpu.VMEM((6 * BAND, TILE), BF)],
        in_specs=[any_spec] * (5 + len(tables)),
        out_specs=[vmem, vmem],
        scratch_shapes=[pltpu.VMEM(x.shape, x.dtype) for x in tables[:-1]]
        + [
            pltpu.VMEM(mask.shape, F32),
            pltpu.VMEM(target.shape, jnp.int32),
            pltpu.VMEM(by_kernel.shape, F32),
            pltpu.SMEM(cond_index.shape, jnp.int32),
            pltpu.SMEM(dose.shape, F32),
            pltpu.VMEM((2, SLABS + 1, BAND, TILE), F32),
            pltpu.VMEM((len(OFFSETS), PACK, TILE), F32),
            pltpu.VMEM((len(OFFSETS), PACK, TILE), F32),
            pltpu.SemaphoreType.DMA((len(tables) + 5,)),
            pltpu.SemaphoreType.DMA((2 * len(OFFSETS) + 1,)),
            pltpu.SemaphoreType.DMA((len(OFFSETS) + 1,)),
        ],
        compiler_params=pltpu.CompilerParams(
            collective_id=0, has_side_effects=True, vmem_limit_bytes=63 * 1024 * 1024
        ),
        name="spectra_and_gradient",
    )(mask, target, by_kernel, cond_index, dose, *tables)
    return pl.pallas_call(
        last_kernel,
        out_shape=jax.ShapeDtypeStruct(mask.shape, F32),
        in_specs=[vmem, vmem],
        out_specs=vmem,
        name="to_pixels",
    )(*[pltpu.with_memory_space_constraint(x, pltpu.VMEM) for x in handed])


def solution(mesh):
    in_specs = (P("row", "col"), P("row", "col"), P("cond"), P(), P())
    out_specs = P("row", "col")
    return jax.shard_map(shards, mesh=mesh, in_specs=in_specs, out_specs=out_specs, check_vma=False)
```

```python
import functools
import math

import jax
import jax.numpy as jnp
import ml_dtypes
import numpy as np
from jax import lax
from jax.experimental import pallas as pl
from jax.experimental.pallas import tpu as pltpu
from jax.sharding import PartitionSpec as P

MESH = pl.DeviceIdType.MESH
BF = jnp.bfloat16
F32 = jnp.float32

TILE = 128
MARGIN = 128
WINDOW = TILE + 2 * MARGIN
BAND = 24
KERNELS = 12
HALF = BAND // 2
REAL = 2 * HALF + 1
PACK = 5
GRID = 48
GROUP = 4
CONDS = 4
OWN = 2
PER_COND = KERNELS // GROUP
SLABS = 2 * OWN * PER_COND
STEEP = 4.0
THRESH = 0.6
OFFSETS = [(-1, -1), (-1, 1), (0, -1), (-1, 0), (1, 0), (0, 1), (1, -1), (1, 1)]
ORDER = [(0, 6, 2), (1, 7, 5), (3, 4)]
ARRIVAL = [3, 4, 5, 1, 7, 2, 0, 6]
FREQ = np.arange(BAND) - HALF
UNIT = 2.0 * math.pi / WINDOW


def parts(table):
    high = table.astype(ml_dtypes.bfloat16)
    low = (table - high.astype(np.float64)).astype(ml_dtypes.bfloat16)
    return high, low


def left3(table):
    high, low = parts(table)
    return np.concatenate([high, high, low], axis=1)


def pair(table):
    return np.stack(parts(table))


def real_basis(positions):
    order = np.arange(HALF + 1)[:, None] * positions[None, :] % WINDOW * UNIT
    return np.concatenate([np.cos(order), np.sin(order)[1:]], axis=0)


def make_tables():
    t = {}
    pixels = np.arange(TILE)
    rows = np.zeros((3, PACK, 8, TILE))
    cols = np.zeros((3, TILE, TILE))
    for d in range(3):
        basis = real_basis(pixels + TILE * (d - 1))
        rows[d, :, :PACK] = basis.reshape(PACK, PACK, TILE)
        for j in range(PACK):
            cols[d, :, REAL * j : REAL * (j + 1)] = basis.T / WINDOW
    t["dft_rows"] = pair(rows.reshape(3 * PACK * 8, TILE))
    for d in range(3):
        t[f"dft_cols{d}"] = pair(cols[d])

    pick = np.zeros((PACK, BAND, 2 * TILE), np.float32)
    spread = np.zeros((2, TILE, 2, GROUP, 32))
    for row, f in enumerate(FREQ):
        a = abs(f)
        j, i = divmod(a, PACK)
        pick[i, row, REAL * j : REAL * (j + 1)] = 1.0
        if f:
            j, i = divmod(HALF + a, PACK)
            pick[i, row, TILE + REAL * j : TILE + REAL * (j + 1)] = np.sign(f)
    for j in range(PACK):
        for col, g in enumerate(FREQ):
            cos_at = REAL * j + abs(g)
            spread[0, cos_at, 0, :, col] = 1.0
            spread[1, cos_at, 1, :, col] = -1.0
            if g:
                sin_at = REAL * j + HALF + abs(g)
                spread[1, sin_at, 0, :, col] = -np.sign(g)
                spread[0, sin_at, 1, :, col] = -np.sign(g)
    t["pick"] = pick
    t["spread"] = spread.reshape(2 * TILE, 2 * TILE).astype(ml_dtypes.bfloat16)

    rows_of = np.zeros((BAND, BAND * BAND), np.float32)
    fold = np.zeros((BAND * BAND, GROUP, 32))
    for l in range(BAND * BAND):
        rows_of[l // BAND, l] = 1.0
        fold[l, :, l % BAND] = 1.0
    t["rows_of"] = rows_of
    t["fold"] = fold.reshape(BAND * BAND, TILE).astype(ml_dtypes.bfloat16)

    angle = FREQ[:, None] * np.arange(GRID)[None, :] % GRID * (2.0 * math.pi / GRID)
    c, s = np.cos(angle), np.sin(angle)
    field_rows = np.block([[c.T, -s.T], [s.T, c.T]])
    t["field_rows"] = left3(field_rows)
    t["field_rows_t"] = left3(field_rows.T)
    field_cols = np.zeros((2, GROUP, 32, 2, GROUP, 64))
    for k in range(GROUP):
        field_cols[0, k, :BAND, 0, k, :GRID] = c
        field_cols[1, k, :BAND, 0, k, :GRID] = -s
        field_cols[0, k, :BAND, 1, k, :GRID] = s
        field_cols[1, k, :BAND, 1, k, :GRID] = c
    field_cols = field_cols.reshape(2 * TILE, 4 * TILE)
    t["field_cols"] = pair(field_cols)
    t["field_cols_t"] = pair(field_cols.T.copy())

    step = WINDOW // GRID
    gap = pixels[:, None] - step * np.arange(GRID)[None, :]
    orders = np.arange(1, GRID // 2)
    inter = (1.0 + 2.0 * np.cos(orders * gap[:, :, None] * UNIT).sum(-1)) / GRID
    inter_wide = np.zeros((TILE, GROUP, 64))
    inter_wide[:, :, :GRID] = inter[:, None, :]
    inter_wide = inter_wide.reshape(TILE, 2 * TILE)
    t["inter_rows"] = left3(inter)
    t["inter_rows_t"] = left3(inter.T)
    t["inter_cols"] = pair(inter_wide.T.copy())
    t["inter_cols_t"] = pair(inter_wide)

    turn = FREQ[:, None] * pixels[None, :] % WINDOW * UNIT
    c, s = np.cos(turn), np.sin(turn)
    last_cols = np.zeros((2, GROUP, 32, 2, TILE))
    last_cols[0, :, :BAND, 0] = c / WINDOW
    last_cols[1, :, :BAND, 0] = -s / WINDOW
    last_cols[0, :, :BAND, 1] = -s / WINDOW
    last_cols[1, :, :BAND, 1] = -c / WINDOW
    t["last_cols"] = pair(last_cols.reshape(2 * TILE, 2 * TILE))
    t["last_rows"] = left3(np.concatenate([c, s], axis=0).T)
    return t


TABLES = make_tables()
NAMES = [
    "dft_rows", "dft_cols0", "dft_cols2", "dft_cols1", "rows_of", "fold", "pick", "spread", "field_rows", "field_cols",
    "inter_cols", "inter_rows", "inter_rows_t", "inter_cols_t", "field_cols_t", "field_rows_t", "last_cols",
    "last_rows",
]

LOADS = ("kernels", "cond", "dose", "rows_of", "fold")


def split(x):
    high = x.astype(BF)
    return high, (x - high.astype(F32)).astype(BF)


def dot(a, b):
    return jnp.dot(a, b, preferred_element_type=F32)


def dot3(x, table):
    high, low = split(x)
    return dot(high, table[0]) + dot(low, table[0]) + dot(high, table[1])


def dot3_in(pieces, x, table):
    rows = x.shape[0] // pieces
    return jnp.concatenate([dot3(x[rows * i : rows * (i + 1)], table) for i in range(pieces)], axis=0)


def stacked3(x):
    high, low = split(x)
    return jnp.concatenate([high, low, high], axis=0)


def main_kernel(*refs):
    n = len(NAMES)
    mask_hbm, target_hbm, kernels_hbm, cond_hbm, dose_hbm = refs[:5]
    tables_hbm = refs[5 : 5 + n]
    table_ref, out_ref = refs[5 + n : 7 + n]
    scratch = refs[7 + n :]
    tab = dict(zip(NAMES, list(scratch[: n - 1]) + [table_ref]))
    mask, target, kernels, cond_ref, dose_ref, kk, sent, held, load_sem, send_sem, recv_sem = scratch[n - 1 :]

    row, col, core = (lax.axis_index(a) for a in ("row", "col", "cond"))
    n_row, n_col = lax.axis_size("row"), lax.axis_size("col")

    copies = {}
    first = [("mask", mask_hbm, mask)] + [(m, s, tab[m]) for m, s in zip(NAMES[:4], tables_hbm[:4])]
    later = (
        [("kernels", kernels_hbm, kernels), ("cond", cond_hbm, cond_ref), ("dose", dose_hbm, dose_ref)]
        + [(m, s, tab[m]) for m, s in zip(NAMES[4:], tables_hbm[4:])]
        + [("target", target_hbm, target)]
    )
    for i, (name, src, dst) in enumerate(first + later):
        copies[name] = pltpu.make_async_copy(src, dst, load_sem.at[i])
    for name, _, _ in first:
        copies[name].start()

    held[...] = jnp.zeros_like(held)
    even = lax.rem(col, 2) == 0

    def from_core(dr, dc, at_row, at_col, at_core):
        return jnp.where((at_row == 0) & (at_col == 0) & (at_core == 0), 0, 1) if dc else 0

    barrier = pltpu.get_barrier_semaphore()
    pl.semaphore_signal(barrier, inc=1, device_id=(row, col, 1 - core), device_id_type=MESH)
    there = []
    count = jnp.int32(1)
    for dr, dc in OFFSETS:
        ok = (row + dr >= 0) & (row + dr < n_row) & (col + dc >= 0) & (col + dc < n_col)
        there.append(ok)
        for to in range(2):
            count = count + jnp.where(ok & (core == from_core(dr, dc, row + dr, col + dc, to)), 1, 0)
        sender = from_core(dr, dc, row, col, core)

        @pl.when(ok)
        def _():
            pl.semaphore_signal(barrier, inc=1, device_id=(row + dr, col + dc, sender), device_id_type=MESH)

    def sending(i, to):
        dr, dc = OFFSETS[i]
        return there[len(OFFSETS) - 1 - i] & (core == from_core(dr, dc, row - dr, col - dc, to))

    for name in ("mask", "dft_rows"):
        copies[name].wait()
    lanes = lax.broadcasted_iota(jnp.int32, (8, TILE), 1)
    table = tab["dft_rows"]
    partial = dot(jnp.concatenate([table[0], table[0], table[1]], axis=1), stacked3(mask[...]))
    partial = split(partial)

    def blocks_of(e):
        copies[f"dft_cols{e}"].wait()
        table = tab[f"dft_cols{e}"]
        products = dot(partial[0], table[0]) + dot(partial[1], table[0]) + dot(partial[0], table[1])
        own = None
        for d in range(3):
            block = None
            for j in range(PACK):
                piece = products[8 * (PACK * d + j) : 8 * (PACK * d + j + 1)]
                block = piece if block is None else jnp.where(lanes < REAL * j, block, piece)
            if d == 1 and e == 1:
                own = block
            else:
                sent[OFFSETS.index((d - 1, e - 1))] = block[:PACK]
        return own

    sends = {}

    def send(order):
        for i in order:
            dr, dc = OFFSETS[i]
            for to in range(2):
                sends[i, to] = pltpu.make_async_remote_copy(
                    src_ref=sent.at[i],
                    dst_ref=held.at[i],
                    send_sem=send_sem.at[2 * i + to],
                    recv_sem=recv_sem.at[i],
                    device_id=(row - dr, col - dc, to),
                    device_id_type=MESH,
                )

                @pl.when(sending(i, to))
                def _():
                    sends[i, to].start()

    blocks_of(0)
    lane = lax.broadcasted_iota(jnp.int32, (BAND, TILE), 1) // 32

    def arrange(step, carry):
        c = step // PER_COND
        group = step - PER_COND * c
        setting = cond_ref[c]
        lines = [kernels[setting, group * GROUP + k, part : part + 1, :] for part in range(2) for k in range(GROUP)]
        folded = []
        for half in (lines[:GROUP], lines[GROUP:]):
            high, low = split(jnp.concatenate([line * tab["rows_of"][...] for line in half], axis=0))
            folded.append(dot(high, tab["fold"][...]) + dot(low, tab["fold"][...]))
        for part in range(2):
            total = folded[part][:BAND]
            for k in range(1, GROUP):
                total = jnp.where(lane == k, folded[part][BAND * k : BAND * (k + 1)], total)
            kk[0, OWN * PER_COND * part + step] = total
        return carry

    def arrange_all():
        for name, _, _ in later:
            copies[name].start()
        for name in LOADS:
            copies[name].wait()
        for c in range(OWN):
            kk[0, SLABS, c : c + 1] = jnp.full((1, TILE), dose_ref[cond_ref[c]], F32)
        lax.fori_loop(0, OWN * PER_COND, arrange, 0)

    ahead = even & ((row > 0) | (col > 0) | (core > 0))
    pl.when(ahead)(arrange_all)

    pl.semaphore_wait(barrier, count)
    send(ORDER[0])
    blocks_of(2)
    send(ORDER[1])
    own = blocks_of(1)
    send(ORDER[2])

    pl.when(jnp.logical_not(ahead))(arrange_all)
    share = pltpu.make_async_remote_copy(
        src_ref=kk.at[0],
        dst_ref=kk.at[1],
        send_sem=send_sem.at[2 * len(OFFSETS)],
        recv_sem=recv_sem.at[len(OFFSETS)],
        device_id=(row, col, 1 - core),
        device_id_type=MESH,
    )
    share.start()

    for name in NAMES[6:] + ["target"]:
        copies[name].wait()
    share.wait_recv()
    goal = target[...].astype(F32)

    z = own[:PACK]
    for i in ARRIVAL:

        @pl.when(there[i])
        def _(i=i):
            sends[i, 0].wait_recv()

        z = z + held[i]
    chosen = None
    for i in range(PACK):
        line = jnp.concatenate([z[i : i + 1], z[i : i + 1]], axis=1)
        piece = line * tab["pick"][i]
        chosen = piece if chosen is None else chosen + piece
    high, low = split(chosen)
    spectrum = dot(high, tab["spread"][...]) + dot(low, tab["spread"][...])
    s_re, s_im = spectrum[:, :TILE], spectrum[:, TILE:]

    def kernel_tile(j):
        who, at = divmod(j, OWN * PER_COND)
        return kk[who, at], kk[who, OWN * PER_COND + at]

    product = []
    for j in range(CONDS * PER_COND):
        k_re, k_im = kernel_tile(j)
        product.append(jnp.concatenate([k_re * s_re - k_im * s_im, k_re * s_im + k_im * s_re], axis=0))
    along = dot(tab["field_rows"][...], stacked3(jnp.concatenate(product, axis=1)))
    along = jnp.concatenate(
        [
            jnp.concatenate([along[:GRID, TILE * j : TILE * (j + 1)], along[GRID:, TILE * j : TILE * (j + 1)]], axis=1)
            for j in range(CONDS * PER_COND)
        ],
        axis=0,
    )
    field = dot3(along, tab["field_cols"])
    square = field * field
    square = square[:, : 2 * TILE] + square[:, 2 * TILE :]
    samples = []
    for c in range(CONDS):
        at = c * PER_COND * GRID
        samples.append(square[at : at + GRID] + square[at + GRID : at + 2 * GRID] + square[at + 2 * GRID : at + 3 * GRID])
    inten = dot3_in(2, jnp.concatenate(samples, axis=0), tab["inter_cols"])
    inten = jnp.concatenate([inten[GRID * c : GRID * (c + 1)] for c in range(CONDS)], axis=1)
    inten = dot(tab["inter_rows"][...], stacked3(inten))
    slopes = []
    for c in range(CONDS):
        scale = kk[c // OWN, SLABS, c % OWN : c % OWN + 1] * (STEEP / (KERNELS * BAND * BAND))
        arg = scale * inten[:, TILE * c : TILE * (c + 1)] - STEEP * THRESH
        e = jnp.exp(-jnp.abs(arg))
        inverse = 1.0 / (1.0 + e)
        resist = jnp.where(arg >= 0, inverse, e * inverse)
        slopes.append((resist - goal) * (e * inverse * inverse) * (4.0 * scale))
    back = dot(tab["inter_rows_t"][...], stacked3(jnp.concatenate(slopes, axis=1)))
    back = jnp.concatenate([back[:, TILE * c : TILE * (c + 1)] for c in range(CONDS)], axis=0)
    weight = dot3_in(2, back, tab["inter_cols_t"])
    pulled = []
    for j in range(CONDS * PER_COND):
        at = j // PER_COND * GRID
        w = weight[at : at + GRID]
        pulled.append(field[GRID * j : GRID * (j + 1)] * jnp.concatenate([w, w], axis=1))
    pulled = dot3_in(2, jnp.concatenate(pulled, axis=0), tab["field_cols_t"])
    pulled = jnp.concatenate(
        [
            jnp.concatenate([pulled[GRID * j : GRID * (j + 1), TILE * p : TILE * (p + 1)] for j in range(CONDS * PER_COND)], axis=1)
            for p in range(2)
        ],
        axis=0,
    )
    pulled = dot(tab["field_rows_t"][...], stacked3(pulled))
    d_re = d_im = None
    for j in range(CONDS * PER_COND):
        k_re, k_im = kernel_tile(j)
        p_re = pulled[:BAND, TILE * j : TILE * (j + 1)]
        p_im = pulled[BAND:, TILE * j : TILE * (j + 1)]
        re, im = k_re * p_re + k_im * p_im, k_re * p_im - k_im * p_re
        d_re, d_im = (re, im) if d_re is None else (d_re + re, d_im + im)
    last = dot3(jnp.concatenate([d_re, d_im], axis=1), tab["last_cols"])
    out_ref[...] = stacked3(jnp.concatenate([last[:, :TILE], last[:, TILE:]], axis=0))
    share.wait_send()
    for i in range(len(OFFSETS)):
        for to in range(2):

            @pl.when(sending(i, to))
            def _(i=i, to=to):
                sends[i, to].wait_send()


def last_kernel(table_ref, sums_ref, out_ref):
    out_ref[...] = dot(table_ref[...], sums_ref[...])


def shards(mask, target, cond_index, kernels, dose):
    any_spec = pl.BlockSpec(memory_space=pl.ANY)
    vmem = pl.BlockSpec(memory_space=pltpu.VMEM)
    tables = [jnp.asarray(TABLES[name]) for name in NAMES]
    by_kernel = jnp.transpose(kernels, (0, 2, 1, 3))
    handed = pl.pallas_call(
        main_kernel,
        out_shape=[pltpu.VMEM(tables[-1].shape, BF), pltpu.VMEM((6 * BAND, TILE), BF)],
        in_specs=[any_spec] * (5 + len(tables)),
        out_specs=[vmem, vmem],
        scratch_shapes=[pltpu.VMEM(x.shape, x.dtype) for x in tables[:-1]]
        + [
            pltpu.VMEM(mask.shape, F32),
            pltpu.VMEM(target.shape, jnp.int32),
            pltpu.VMEM(by_kernel.shape, F32),
            pltpu.SMEM(cond_index.shape, jnp.int32),
            pltpu.SMEM(dose.shape, F32),
            pltpu.VMEM((2, SLABS + 1, BAND, TILE), F32),
            pltpu.VMEM((len(OFFSETS), PACK, TILE), F32),
            pltpu.VMEM((len(OFFSETS), PACK, TILE), F32),
            pltpu.SemaphoreType.DMA((len(tables) + 5,)),
            pltpu.SemaphoreType.DMA((2 * len(OFFSETS) + 1,)),
            pltpu.SemaphoreType.DMA((len(OFFSETS) + 1,)),
        ],
        compiler_params=pltpu.CompilerParams(
            collective_id=0, has_side_effects=True, vmem_limit_bytes=63 * 1024 * 1024
        ),
        name="spectra_and_gradient",
    )(mask, target, by_kernel, cond_index, dose, *tables)
    return pl.pallas_call(
        last_kernel,
        out_shape=jax.ShapeDtypeStruct(mask.shape, F32),
        in_specs=[vmem, vmem],
        out_specs=vmem,
        name="to_pixels",
    )(*[pltpu.with_memory_space_constraint(x, pltpu.VMEM) for x in handed])


def solution(mesh):
    in_specs = (P("row", "col"), P("row", "col"), P("cond"), P(), P())
    out_specs = P("row", "col")
    return jax.shard_map(shards, mesh=mesh, in_specs=in_specs, out_specs=out_specs, check_vma=False)
```

```python
import functools
import math

import jax
import jax.numpy as jnp
import ml_dtypes
import numpy as np
from jax import lax
from jax.experimental import pallas as pl
from jax.experimental.pallas import tpu as pltpu
from jax.sharding import PartitionSpec as P

MESH = pl.DeviceIdType.MESH
BF = jnp.bfloat16
F32 = jnp.float32

TILE = 128
MARGIN = 128
WINDOW = TILE + 2 * MARGIN
BAND = 24
KERNELS = 12
HALF = BAND // 2
REAL = 2 * HALF + 1
PACK = 5
GRID = 48
GROUP = 4
CONDS = 4
OWN = 2
PER_COND = KERNELS // GROUP
SLABS = 2 * OWN * PER_COND
STEEP = 4.0
THRESH = 0.6
OFFSETS = [(-1, -1), (-1, 1), (0, -1), (-1, 0), (1, 0), (0, 1), (1, -1), (1, 1)]
ORDER = [(0, 6, 2), (1, 7, 5), (3, 4)]
ARRIVAL = [3, 4, 5, 1, 7, 2, 0, 6]
FREQ = np.arange(BAND) - HALF
UNIT = 2.0 * math.pi / WINDOW


def parts(table):
    high = table.astype(ml_dtypes.bfloat16)
    low = (table - high.astype(np.float64)).astype(ml_dtypes.bfloat16)
    return high, low


def left3(table):
    high, low = parts(table)
    return np.concatenate([high, high, low], axis=1)


def pair(table):
    return np.stack(parts(table))


def real_basis(positions):
    order = np.arange(HALF + 1)[:, None] * positions[None, :] % WINDOW * UNIT
    return np.concatenate([np.cos(order), np.sin(order)[1:]], axis=0)


def make_tables():
    t = {}
    pixels = np.arange(TILE)
    rows = np.zeros((3, PACK, 8, TILE))
    cols = np.zeros((3, TILE, TILE))
    for d in range(3):
        basis = real_basis(pixels + TILE * (d - 1))
        rows[d, :, :PACK] = basis.reshape(PACK, PACK, TILE)
        for j in range(PACK):
            cols[d, :, REAL * j : REAL * (j + 1)] = basis.T / WINDOW
    t["dft_rows"] = pair(np.pad(rows.reshape(3 * PACK * 8, TILE), ((0, 8), (0, 0))))
    for d in range(3):
        t[f"dft_cols{d}"] = pair(cols[d])

    pick = np.zeros((PACK, BAND, 2 * TILE), np.float32)
    spread = np.zeros((2, TILE, 2, GROUP, 32))
    for row, f in enumerate(FREQ):
        a = abs(f)
        j, i = divmod(a, PACK)
        pick[i, row, REAL * j : REAL * (j + 1)] = 1.0
        if f:
            j, i = divmod(HALF + a, PACK)
            pick[i, row, TILE + REAL * j : TILE + REAL * (j + 1)] = np.sign(f)
    for j in range(PACK):
        for col, g in enumerate(FREQ):
            cos_at = REAL * j + abs(g)
            spread[0, cos_at, 0, :, col] = 1.0
            spread[1, cos_at, 1, :, col] = -1.0
            if g:
                sin_at = REAL * j + HALF + abs(g)
                spread[1, sin_at, 0, :, col] = -np.sign(g)
                spread[0, sin_at, 1, :, col] = -np.sign(g)
    t["pick"] = pick
    t["spread"] = spread.reshape(2 * TILE, 2 * TILE).astype(ml_dtypes.bfloat16)

    rows_of = np.zeros((BAND, BAND * BAND), np.float32)
    fold = np.zeros((BAND * BAND, GROUP, 32))
    for l in range(BAND * BAND):
        rows_of[l // BAND, l] = 1.0
        fold[l, :, l % BAND] = 1.0
    t["rows_of"] = rows_of
    t["fold"] = fold.reshape(BAND * BAND, TILE).astype(ml_dtypes.bfloat16)

    angle = FREQ[:, None] * np.arange(GRID)[None, :] % GRID * (2.0 * math.pi / GRID)
    c, s = np.cos(angle), np.sin(angle)
    field_rows = np.block([[c.T, -s.T], [s.T, c.T]])
    t["field_rows"] = left3(field_rows)
    t["field_rows_t"] = left3(field_rows.T)
    field_cols = np.zeros((2, GROUP, 32, 2, GROUP, 64))
    for k in range(GROUP):
        field_cols[0, k, :BAND, 0, k, :GRID] = c
        field_cols[1, k, :BAND, 0, k, :GRID] = -s
        field_cols[0, k, :BAND, 1, k, :GRID] = s
        field_cols[1, k, :BAND, 1, k, :GRID] = c
    field_cols = field_cols.reshape(2 * TILE, 4 * TILE)
    t["field_cols"] = pair(field_cols)
    t["field_cols_t"] = pair(field_cols.T.copy())

    step = WINDOW // GRID
    gap = pixels[:, None] - step * np.arange(GRID)[None, :]
    orders = np.arange(1, GRID // 2)
    inter = (1.0 + 2.0 * np.cos(orders * gap[:, :, None] * UNIT).sum(-1)) / GRID
    inter_wide = np.zeros((TILE, GROUP, 64))
    inter_wide[:, :, :GRID] = inter[:, None, :]
    inter_wide = inter_wide.reshape(TILE, 2 * TILE)
    t["inter_rows"] = left3(inter)
    t["inter_rows_t"] = left3(inter.T)
    t["inter_cols"] = pair(inter_wide.T.copy())
    t["inter_cols_t"] = pair(inter_wide)

    turn = FREQ[:, None] * pixels[None, :] % WINDOW * UNIT
    c, s = np.cos(turn), np.sin(turn)
    last_cols = np.zeros((2, GROUP, 32, 2, TILE))
    last_cols[0, :, :BAND, 0] = c / WINDOW
    last_cols[1, :, :BAND, 0] = -s / WINDOW
    last_cols[0, :, :BAND, 1] = -s / WINDOW
    last_cols[1, :, :BAND, 1] = -c / WINDOW
    t["last_cols"] = pair(last_cols.reshape(2 * TILE, 2 * TILE))
    t["last_rows"] = left3(np.concatenate([c, s], axis=0).T)
    return t


TABLES = make_tables()
NAMES = [
    "dft_rows", "dft_cols0", "dft_cols2", "dft_cols1", "rows_of", "fold", "pick", "spread", "field_rows", "field_cols",
    "inter_cols", "inter_rows", "inter_rows_t", "inter_cols_t", "field_cols_t", "field_rows_t", "last_cols",
    "last_rows",
]

LOADS = ("kernels", "cond", "dose", "rows_of", "fold")


def split(x):
    high = x.astype(BF)
    return high, (x - high.astype(F32)).astype(BF)


def dot(a, b):
    return jnp.dot(a, b, preferred_element_type=F32)


def dot3(x, table):
    high, low = split(x)
    return dot(high, table[0]) + dot(low, table[0]) + dot(high, table[1])


def dot3_in(pieces, x, table):
    rows = x.shape[0] // pieces
    return jnp.concatenate([dot3(x[rows * i : rows * (i + 1)], table) for i in range(pieces)], axis=0)


def stacked3(x):
    high, low = split(x)
    return jnp.concatenate([high, low, high], axis=0)


def main_kernel(*refs):
    n = len(NAMES)
    mask_hbm, target_hbm, kernels_hbm, cond_hbm, dose_hbm = refs[:5]
    tables_hbm = refs[5 : 5 + n]
    table_ref, out_ref = refs[5 + n : 7 + n]
    scratch = refs[7 + n :]
    tab = dict(zip(NAMES, list(scratch[: n - 1]) + [table_ref]))
    mask, target, kernels, cond_ref, dose_ref, kk, sent, held, load_sem, send_sem, recv_sem = scratch[n - 1 :]

    row, col, core = (lax.axis_index(a) for a in ("row", "col", "cond"))
    n_row, n_col = lax.axis_size("row"), lax.axis_size("col")

    copies = {}
    first = [("mask", mask_hbm, mask)] + [(m, s, tab[m]) for m, s in zip(NAMES[:4], tables_hbm[:4])]
    later = (
        [("kernels", kernels_hbm, kernels), ("cond", cond_hbm, cond_ref), ("dose", dose_hbm, dose_ref)]
        + [(m, s, tab[m]) for m, s in zip(NAMES[4:], tables_hbm[4:])]
        + [("target", target_hbm, target)]
    )
    for i, (name, src, dst) in enumerate(first + later):
        copies[name] = pltpu.make_async_copy(src, dst, load_sem.at[i])
    for name, _, _ in first:
        copies[name].start()

    held[...] = jnp.zeros_like(held)
    even = lax.rem(col, 2) == 0

    def from_core(dr, dc, at_row, at_col, at_core):
        return jnp.where((at_row == 0) & (at_col == 0) & (at_core == 0), 0, 1) if dc else 0

    barrier = pltpu.get_barrier_semaphore()
    pl.semaphore_signal(barrier, inc=1, device_id=(row, col, 1 - core), device_id_type=MESH)
    there = []
    count = jnp.int32(1)
    for dr, dc in OFFSETS:
        ok = (row + dr >= 0) & (row + dr < n_row) & (col + dc >= 0) & (col + dc < n_col)
        there.append(ok)
        for to in range(2):
            count = count + jnp.where(ok & (core == from_core(dr, dc, row + dr, col + dc, to)), 1, 0)
        sender = from_core(dr, dc, row, col, core)

        @pl.when(ok)
        def _():
            pl.semaphore_signal(barrier, inc=1, device_id=(row + dr, col + dc, sender), device_id_type=MESH)

    def sending(i, to):
        dr, dc = OFFSETS[i]
        return there[len(OFFSETS) - 1 - i] & (core == from_core(dr, dc, row - dr, col - dc, to))

    for name in ("mask", "dft_rows"):
        copies[name].wait()
    lanes = lax.broadcasted_iota(jnp.int32, (8, TILE), 1)
    table = tab["dft_rows"]
    partial = dot(jnp.concatenate([table[0], table[0], table[1]], axis=1), stacked3(mask[...]))
    partial = split(partial)

    def blocks_of(e):
        copies[f"dft_cols{e}"].wait()
        table = tab[f"dft_cols{e}"]
        products = dot(partial[0], table[0]) + dot(partial[1], table[0]) + dot(partial[0], table[1])
        own = None
        for d in range(3):
            block = None
            for j in range(PACK):
                piece = products[8 * (PACK * d + j) : 8 * (PACK * d + j + 1)]
                block = piece if block is None else jnp.where(lanes < REAL * j, block, piece)
            if d == 1 and e == 1:
                own = block
            else:
                sent[OFFSETS.index((d - 1, e - 1))] = block[:PACK]
        return own

    sends = {}

    def send(order):
        for i in order:
            dr, dc = OFFSETS[i]
            for to in range(2):
                sends[i, to] = pltpu.make_async_remote_copy(
                    src_ref=sent.at[i],
                    dst_ref=held.at[i],
                    send_sem=send_sem.at[2 * i + to],
                    recv_sem=recv_sem.at[i],
                    device_id=(row - dr, col - dc, to),
                    device_id_type=MESH,
                )

                @pl.when(sending(i, to))
                def _():
                    sends[i, to].start()

    blocks_of(0)
    lane = lax.broadcasted_iota(jnp.int32, (BAND, TILE), 1) // 32

    def arrange(step, carry):
        c = step // PER_COND
        group = step - PER_COND * c
        setting = cond_ref[c]
        lines = [kernels[setting, group * GROUP + k, part : part + 1, :] for part in range(2) for k in range(GROUP)]
        folded = []
        for half in (lines[:GROUP], lines[GROUP:]):
            high, low = split(jnp.concatenate([line * tab["rows_of"][...] for line in half], axis=0))
            folded.append(dot(high, tab["fold"][...]) + dot(low, tab["fold"][...]))
        for part in range(2):
            total = folded[part][:BAND]
            for k in range(1, GROUP):
                total = jnp.where(lane == k, folded[part][BAND * k : BAND * (k + 1)], total)
            kk[0, OWN * PER_COND * part + step] = total
        return carry

    def arrange_all():
        for name, _, _ in later:
            copies[name].start()
        for name in LOADS:
            copies[name].wait()
        for c in range(OWN):
            kk[0, SLABS, c : c + 1] = jnp.full((1, TILE), dose_ref[cond_ref[c]], F32)
        lax.fori_loop(0, OWN * PER_COND, arrange, 0)

    ahead = even & ((row > 0) | (col > 0) | (core > 0))
    pl.when(ahead)(arrange_all)

    pl.semaphore_wait(barrier, count)
    send(ORDER[0])
    blocks_of(2)
    send(ORDER[1])
    own = blocks_of(1)
    send(ORDER[2])

    pl.when(jnp.logical_not(ahead))(arrange_all)
    share = pltpu.make_async_remote_copy(
        src_ref=kk.at[0],
        dst_ref=kk.at[1],
        send_sem=send_sem.at[2 * len(OFFSETS)],
        recv_sem=recv_sem.at[len(OFFSETS)],
        device_id=(row, col, 1 - core),
        device_id_type=MESH,
    )
    share.start()

    for name in NAMES[6:] + ["target"]:
        copies[name].wait()
    share.wait_recv()
    goal = target[...].astype(F32)

    z = own[:PACK]
    for i in ARRIVAL:

        @pl.when(there[i])
        def _(i=i):
            sends[i, 0].wait_recv()

        z = z + held[i]
    chosen = None
    for i in range(PACK):
        line = jnp.concatenate([z[i : i + 1], z[i : i + 1]], axis=1)
        piece = line * tab["pick"][i]
        chosen = piece if chosen is None else chosen + piece
    high, low = split(chosen)
    spectrum = dot(high, tab["spread"][...]) + dot(low, tab["spread"][...])
    s_re, s_im = spectrum[:, :TILE], spectrum[:, TILE:]

    def kernel_tile(j):
        who, at = divmod(j, OWN * PER_COND)
        return kk[who, at], kk[who, OWN * PER_COND + at]

    product = []
    for j in range(CONDS * PER_COND):
        k_re, k_im = kernel_tile(j)
        product.append(jnp.concatenate([k_re * s_re - k_im * s_im, k_re * s_im + k_im * s_re], axis=0))
    along = dot(tab["field_rows"][...], stacked3(jnp.concatenate(product, axis=1)))
    along = jnp.concatenate(
        [
            jnp.concatenate([along[:GRID, TILE * j : TILE * (j + 1)], along[GRID:, TILE * j : TILE * (j + 1)]], axis=1)
            for j in range(CONDS * PER_COND)
        ],
        axis=0,
    )
    field = dot3(along, tab["field_cols"])
    square = field * field
    square = square[:, : 2 * TILE] + square[:, 2 * TILE :]
    samples = []
    for c in range(CONDS):
        at = c * PER_COND * GRID
        samples.append(square[at : at + GRID] + square[at + GRID : at + 2 * GRID] + square[at + 2 * GRID : at + 3 * GRID])
    inten = dot3_in(2, jnp.concatenate(samples, axis=0), tab["inter_cols"])
    inten = jnp.concatenate([inten[GRID * c : GRID * (c + 1)] for c in range(CONDS)], axis=1)
    inten = dot(tab["inter_rows"][...], stacked3(inten))
    slopes = []
    for c in range(CONDS):
        scale = kk[c // OWN, SLABS, c % OWN : c % OWN + 1] * (STEEP / (KERNELS * BAND * BAND))
        arg = scale * inten[:, TILE * c : TILE * (c + 1)] - STEEP * THRESH
        e = jnp.exp(-jnp.abs(arg))
        inverse = 1.0 / (1.0 + e)
        resist = jnp.where(arg >= 0, inverse, e * inverse)
        slopes.append((resist - goal) * (e * inverse * inverse) * (4.0 * scale))
    back = dot(tab["inter_rows_t"][...], stacked3(jnp.concatenate(slopes, axis=1)))
    back = jnp.concatenate([back[:, TILE * c : TILE * (c + 1)] for c in range(CONDS)], axis=0)
    weight = dot3_in(2, back, tab["inter_cols_t"])
    pulled = []
    for j in range(CONDS * PER_COND):
        at = j // PER_COND * GRID
        w = weight[at : at + GRID]
        pulled.append(field[GRID * j : GRID * (j + 1)] * jnp.concatenate([w, w], axis=1))
    pulled = dot3_in(2, jnp.concatenate(pulled, axis=0), tab["field_cols_t"])
    pulled = jnp.concatenate(
        [
            jnp.concatenate([pulled[GRID * j : GRID * (j + 1), TILE * p : TILE * (p + 1)] for j in range(CONDS * PER_COND)], axis=1)
            for p in range(2)
        ],
        axis=0,
    )
    pulled = dot(tab["field_rows_t"][...], stacked3(pulled))
    d_re = d_im = None
    for j in range(CONDS * PER_COND):
        k_re, k_im = kernel_tile(j)
        p_re = pulled[:BAND, TILE * j : TILE * (j + 1)]
        p_im = pulled[BAND:, TILE * j : TILE * (j + 1)]
        re, im = k_re * p_re + k_im * p_im, k_re * p_im - k_im * p_re
        d_re, d_im = (re, im) if d_re is None else (d_re + re, d_im + im)
    last = dot3(jnp.concatenate([d_re, d_im], axis=1), tab["last_cols"])
    out_ref[...] = stacked3(jnp.concatenate([last[:, :TILE], last[:, TILE:]], axis=0))
    share.wait_send()
    for i in range(len(OFFSETS)):
        for to in range(2):

            @pl.when(sending(i, to))
            def _(i=i, to=to):
                sends[i, to].wait_send()


def last_kernel(table_ref, sums_ref, out_ref):
    out_ref[...] = dot(table_ref[...], sums_ref[...])


def shards(mask, target, cond_index, kernels, dose):
    any_spec = pl.BlockSpec(memory_space=pl.ANY)
    vmem = pl.BlockSpec(memory_space=pltpu.VMEM)
    tables = [jnp.asarray(TABLES[name]) for name in NAMES]
    by_kernel = jnp.transpose(kernels, (0, 2, 1, 3))
    handed = pl.pallas_call(
        main_kernel,
        out_shape=[pltpu.VMEM(tables[-1].shape, BF), pltpu.VMEM((6 * BAND, TILE), BF)],
        in_specs=[any_spec] * (5 + len(tables)),
        out_specs=[vmem, vmem],
        scratch_shapes=[pltpu.VMEM(x.shape, x.dtype) for x in tables[:-1]]
        + [
            pltpu.VMEM(mask.shape, F32),
            pltpu.VMEM(target.shape, jnp.int32),
            pltpu.VMEM(by_kernel.shape, F32),
            pltpu.SMEM(cond_index.shape, jnp.int32),
            pltpu.SMEM(dose.shape, F32),
            pltpu.VMEM((2, SLABS + 1, BAND, TILE), F32),
            pltpu.VMEM((len(OFFSETS), PACK, TILE), F32),
            pltpu.VMEM((len(OFFSETS), PACK, TILE), F32),
            pltpu.SemaphoreType.DMA((len(tables) + 5,)),
            pltpu.SemaphoreType.DMA((2 * len(OFFSETS) + 1,)),
            pltpu.SemaphoreType.DMA((len(OFFSETS) + 1,)),
        ],
        compiler_params=pltpu.CompilerParams(
            collective_id=0, has_side_effects=True, vmem_limit_bytes=63 * 1024 * 1024
        ),
        name="spectra_and_gradient",
    )(mask, target, by_kernel, cond_index, dose, *tables)
    return pl.pallas_call(
        last_kernel,
        out_shape=jax.ShapeDtypeStruct(mask.shape, F32),
        in_specs=[vmem, vmem],
        out_specs=vmem,
        name="to_pixels",
    )(*[pltpu.with_memory_space_constraint(x, pltpu.VMEM) for x in handed])


def solution(mesh):
    in_specs = (P("row", "col"), P("row", "col"), P("cond"), P(), P())
    out_specs = P("row", "col")
    return jax.shard_map(shards, mesh=mesh, in_specs=in_specs, out_specs=out_specs, check_vma=False)
```

```python
import functools
import math

import jax
import jax.numpy as jnp
import ml_dtypes
import numpy as np
from jax import lax
from jax.experimental import pallas as pl
from jax.experimental.pallas import tpu as pltpu
from jax.sharding import PartitionSpec as P

MESH = pl.DeviceIdType.MESH
BF = jnp.bfloat16
F32 = jnp.float32

TILE = 128
MARGIN = 128
WINDOW = TILE + 2 * MARGIN
BAND = 24
KERNELS = 12
HALF = BAND // 2
REAL = 2 * HALF + 1
PACK = 5
GRID = 48
GROUP = 4
CONDS = 4
OWN = 2
PER_COND = KERNELS // GROUP
SLABS = 2 * OWN * PER_COND
STEEP = 4.0
THRESH = 0.6
OFFSETS = [(-1, -1), (-1, 1), (0, -1), (-1, 0), (1, 0), (0, 1), (1, -1), (1, 1)]
ORDER = [(0, 6, 2), (1, 7, 5), (3, 4)]
ARRIVAL = [3, 4, 5, 1, 7, 2, 0, 6]
FREQ = np.arange(BAND) - HALF
UNIT = 2.0 * math.pi / WINDOW


def parts(table):
    high = table.astype(ml_dtypes.bfloat16)
    low = (table - high.astype(np.float64)).astype(ml_dtypes.bfloat16)
    return high, low


def left3(table):
    high, low = parts(table)
    return np.concatenate([high, high, low], axis=1)


def pair(table):
    return np.stack(parts(table))


def real_basis(positions):
    order = np.arange(HALF + 1)[:, None] * positions[None, :] % WINDOW * UNIT
    return np.concatenate([np.cos(order), np.sin(order)[1:]], axis=0)


def make_tables():
    t = {}
    pixels = np.arange(TILE)
    rows = np.zeros((3, PACK, 8, TILE))
    cols = np.zeros((3, TILE, TILE))
    for d in range(3):
        basis = real_basis(pixels + TILE * (d - 1))
        rows[d, :, :PACK] = basis.reshape(PACK, PACK, TILE)
        for j in range(PACK):
            cols[d, :, REAL * j : REAL * (j + 1)] = basis.T / WINDOW
    t["dft_rows"] = pair(np.pad(rows.reshape(3 * PACK * 8, TILE), ((0, 8), (0, 0))))
    for d in range(3):
        t[f"dft_cols{d}"] = pair(cols[d])

    pick = np.zeros((PACK, BAND, 2 * TILE), np.float32)
    spread = np.zeros((2, TILE, 2, GROUP, 32))
    for row, f in enumerate(FREQ):
        a = abs(f)
        j, i = divmod(a, PACK)
        pick[i, row, REAL * j : REAL * (j + 1)] = 1.0
        if f:
            j, i = divmod(HALF + a, PACK)
            pick[i, row, TILE + REAL * j : TILE + REAL * (j + 1)] = np.sign(f)
    for j in range(PACK):
        for col, g in enumerate(FREQ):
            cos_at = REAL * j + abs(g)
            spread[0, cos_at, 0, :, col] = 1.0
            spread[1, cos_at, 1, :, col] = -1.0
            if g:
                sin_at = REAL * j + HALF + abs(g)
                spread[1, sin_at, 0, :, col] = -np.sign(g)
                spread[0, sin_at, 1, :, col] = -np.sign(g)
    t["pick"] = pick
    t["spread"] = spread.reshape(2 * TILE, 2 * TILE).astype(ml_dtypes.bfloat16)

    rows_of = np.zeros((BAND, BAND * BAND), np.float32)
    fold = np.zeros((BAND * BAND, GROUP, 32))
    for l in range(BAND * BAND):
        rows_of[l // BAND, l] = 1.0
        fold[l, :, l % BAND] = 1.0
    t["rows_of"] = rows_of
    t["fold"] = fold.reshape(BAND * BAND, TILE).astype(ml_dtypes.bfloat16)

    angle = FREQ[:, None] * np.arange(GRID)[None, :] % GRID * (2.0 * math.pi / GRID)
    c, s = np.cos(angle), np.sin(angle)
    field_rows = np.block([[c.T, -s.T], [s.T, c.T]])
    t["field_rows"] = left3(field_rows)
    t["field_rows_t"] = left3(field_rows.T)
    field_cols = np.zeros((2, GROUP, 32, 2, GROUP, 64))
    for k in range(GROUP):
        field_cols[0, k, :BAND, 0, k, :GRID] = c
        field_cols[1, k, :BAND, 0, k, :GRID] = -s
        field_cols[0, k, :BAND, 1, k, :GRID] = s
        field_cols[1, k, :BAND, 1, k, :GRID] = c
    field_cols = field_cols.reshape(2 * TILE, 4 * TILE)
    t["field_cols"] = pair(field_cols)
    t["field_cols_t"] = pair(field_cols.T.copy())

    step = WINDOW // GRID
    gap = pixels[:, None] - step * np.arange(GRID)[None, :]
    orders = np.arange(1, GRID // 2)
    inter = (1.0 + 2.0 * np.cos(orders * gap[:, :, None] * UNIT).sum(-1)) / GRID
    inter_wide = np.zeros((TILE, GROUP, 64))
    inter_wide[:, :, :GRID] = inter[:, None, :]
    inter_wide = inter_wide.reshape(TILE, 2 * TILE)
    t["inter_rows"] = left3(inter)
    t["inter_rows_t"] = left3(inter.T)
    t["inter_cols"] = pair(inter_wide.T.copy())
    t["inter_cols_t"] = pair(inter_wide)

    turn = FREQ[:, None] * pixels[None, :] % WINDOW * UNIT
    c, s = np.cos(turn), np.sin(turn)
    last_cols = np.zeros((2, GROUP, 32, 2, TILE))
    last_cols[0, :, :BAND, 0] = c / WINDOW
    last_cols[1, :, :BAND, 0] = -s / WINDOW
    last_cols[0, :, :BAND, 1] = -s / WINDOW
    last_cols[1, :, :BAND, 1] = -c / WINDOW
    t["last_cols"] = pair(last_cols.reshape(2 * TILE, 2 * TILE))
    t["last_rows"] = left3(np.concatenate([c, s], axis=0).T)
    return t


TABLES = make_tables()
NAMES = [
    "dft_rows", "dft_cols0", "dft_cols2", "dft_cols1", "rows_of", "fold", "pick", "spread", "field_rows", "field_cols",
    "inter_cols", "inter_rows", "inter_rows_t", "inter_cols_t", "field_cols_t", "field_rows_t", "last_cols",
    "last_rows",
]

LOADS = ("kernels", "cond", "dose", "rows_of", "fold")


def split(x):
    high = x.astype(BF)
    return high, (x - high.astype(F32)).astype(BF)


def dot(a, b):
    return jnp.dot(a, b, preferred_element_type=F32)


def dot3(x, table):
    high, low = split(x)
    return dot(high, table[0]) + dot(low, table[0]) + dot(high, table[1])


def dot3_in(pieces, x, table):
    rows = x.shape[0] // pieces
    return jnp.concatenate([dot3(x[rows * i : rows * (i + 1)], table) for i in range(pieces)], axis=0)


def stacked3(x):
    high, low = split(x)
    return jnp.concatenate([high, low, high], axis=0)


def main_kernel(*refs):
    n = len(NAMES)
    mask_hbm, target_hbm, kernels_hbm, cond_hbm, dose_hbm = refs[:5]
    tables_hbm = refs[5 : 5 + n]
    table_ref, out_ref = refs[5 + n : 7 + n]
    scratch = refs[7 + n :]
    tab = dict(zip(NAMES, list(scratch[: n - 1]) + [table_ref]))
    mask, target, kernels, cond_ref, dose_ref, kk, sent, held, load_sem, send_sem, recv_sem = scratch[n - 1 :]

    row, col, core = (lax.axis_index(a) for a in ("row", "col", "cond"))
    n_row, n_col = lax.axis_size("row"), lax.axis_size("col")

    copies = {}
    first = [("mask", mask_hbm, mask)] + [(m, s, tab[m]) for m, s in zip(NAMES[:4], tables_hbm[:4])]
    later = (
        [("kernels", kernels_hbm, kernels), ("cond", cond_hbm, cond_ref), ("dose", dose_hbm, dose_ref)]
        + [(m, s, tab[m]) for m, s in zip(NAMES[4:], tables_hbm[4:])]
        + [("target", target_hbm, target)]
    )
    for i, (name, src, dst) in enumerate(first + later):
        copies[name] = pltpu.make_async_copy(src, dst, load_sem.at[i])
    for name, _, _ in first:
        copies[name].start()

    held[...] = jnp.zeros_like(held)
    even = lax.rem(col, 2) == 0

    def from_core(dr, dc, at_row, at_col, at_core):
        return jnp.where((at_row == 0) & (at_col == 0) & (at_core == 0), 0, 1) if dc else 0

    barrier = pltpu.get_barrier_semaphore()
    pl.semaphore_signal(barrier, inc=1, device_id=(row, col, 1 - core), device_id_type=MESH)
    there = []
    count = jnp.int32(1)
    for dr, dc in OFFSETS:
        ok = (row + dr >= 0) & (row + dr < n_row) & (col + dc >= 0) & (col + dc < n_col)
        there.append(ok)
        for to in range(2):
            count = count + jnp.where(ok & (core == from_core(dr, dc, row + dr, col + dc, to)), 1, 0)
        sender = from_core(dr, dc, row, col, core)

        @pl.when(ok)
        def _():
            pl.semaphore_signal(barrier, inc=1, device_id=(row + dr, col + dc, sender), device_id_type=MESH)

    def sending(i, to):
        dr, dc = OFFSETS[i]
        return there[len(OFFSETS) - 1 - i] & (core == from_core(dr, dc, row - dr, col - dc, to))

    for name in ("mask", "dft_rows"):
        copies[name].wait()
    lanes = lax.broadcasted_iota(jnp.int32, (8, TILE), 1)
    table = tab["dft_rows"]
    partial = dot(jnp.concatenate([table[0], table[0], table[1]], axis=1), stacked3(mask[...]))
    partial = split(partial)

    def blocks_of(e):
        copies[f"dft_cols{e}"].wait()
        table = tab[f"dft_cols{e}"]
        products = dot(partial[0], table[0]) + dot(partial[1], table[0]) + dot(partial[0], table[1])
        own = None
        for d in range(3):
            block = None
            for j in range(PACK):
                piece = products[8 * (PACK * d + j) : 8 * (PACK * d + j + 1)]
                block = piece if block is None else jnp.where(lanes < REAL * j, block, piece)
            if d == 1 and e == 1:
                own = block
            else:
                sent[OFFSETS.index((d - 1, e - 1))] = block[:PACK]
        return own

    sends = {}

    def send(order):
        for i in order:
            dr, dc = OFFSETS[i]
            for to in range(2):
                sends[i, to] = pltpu.make_async_remote_copy(
                    src_ref=sent.at[i],
                    dst_ref=held.at[i],
                    send_sem=send_sem.at[2 * i + to],
                    recv_sem=recv_sem.at[i],
                    device_id=(row - dr, col - dc, to),
                    device_id_type=MESH,
                )

                @pl.when(sending(i, to))
                def _():
                    sends[i, to].start()

    blocks_of(0)
    lane = lax.broadcasted_iota(jnp.int32, (BAND, TILE), 1) // 32

    def arrange(step, carry):
        c = step // PER_COND
        group = step - PER_COND * c
        setting = cond_ref[c]
        lines = [kernels[setting, group * GROUP + k, part : part + 1, :] for part in range(2) for k in range(GROUP)]
        folded = []
        for half in (lines[:GROUP], lines[GROUP:]):
            high, low = split(jnp.concatenate([line * tab["rows_of"][...] for line in half], axis=0))
            folded.append(dot(high, tab["fold"][...]) + dot(low, tab["fold"][...]))
        for part in range(2):
            total = folded[part][:BAND]
            for k in range(1, GROUP):
                total = jnp.where(lane == k, folded[part][BAND * k : BAND * (k + 1)], total)
            kk[0, OWN * PER_COND * part + step] = total
        return carry

    def arrange_all():
        for name, _, _ in later:
            copies[name].start()
        for name in LOADS:
            copies[name].wait()
        for c in range(OWN):
            kk[0, SLABS, c : c + 1] = jnp.full((1, TILE), dose_ref[cond_ref[c]], F32)
        lax.fori_loop(0, OWN * PER_COND, arrange, 0)

    ahead = even & ((row > 0) | (col > 0) | (core > 0))
    pl.when(ahead)(arrange_all)

    pl.semaphore_wait(barrier, count)
    send(ORDER[0])
    blocks_of(2)
    send(ORDER[1])
    own = blocks_of(1)
    send(ORDER[2])

    pl.when(jnp.logical_not(ahead))(arrange_all)
    share = pltpu.make_async_remote_copy(
        src_ref=kk.at[0],
        dst_ref=kk.at[1],
        send_sem=send_sem.at[2 * len(OFFSETS)],
        recv_sem=recv_sem.at[len(OFFSETS)],
        device_id=(row, col, 1 - core),
        device_id_type=MESH,
    )
    share.start()

    for name in NAMES[6:] + ["target"]:
        copies[name].wait()
    share.wait_recv()
    goal = target[...].astype(F32)

    for i in range(len(OFFSETS)):
        for to in range(2):

            @pl.when(sending(i, to))
            def _(i=i, to=to):
                sends[i, to].wait_send()

    z = own[:PACK]
    for i in ARRIVAL:

        @pl.when(there[i])
        def _(i=i):
            sends[i, 0].wait_recv()

        z = z + held[i]
    chosen = None
    for i in range(PACK):
        line = jnp.concatenate([z[i : i + 1], z[i : i + 1]], axis=1)
        piece = line * tab["pick"][i]
        chosen = piece if chosen is None else chosen + piece
    high, low = split(chosen)
    spectrum = dot(high, tab["spread"][...]) + dot(low, tab["spread"][...])
    s_re, s_im = spectrum[:, :TILE], spectrum[:, TILE:]

    def kernel_tile(j):
        who, at = divmod(j, OWN * PER_COND)
        return kk[who, at], kk[who, OWN * PER_COND + at]

    product = []
    for j in range(CONDS * PER_COND):
        k_re, k_im = kernel_tile(j)
        product.append(jnp.concatenate([k_re * s_re - k_im * s_im, k_re * s_im + k_im * s_re], axis=0))
    along = dot(tab["field_rows"][...], stacked3(jnp.concatenate(product, axis=1)))
    along = jnp.concatenate(
        [
            jnp.concatenate([along[:GRID, TILE * j : TILE * (j + 1)], along[GRID:, TILE * j : TILE * (j + 1)]], axis=1)
            for j in range(CONDS * PER_COND)
        ],
        axis=0,
    )
    field = dot3(along, tab["field_cols"])
    square = field * field
    square = square[:, : 2 * TILE] + square[:, 2 * TILE :]
    samples = []
    for c in range(CONDS):
        at = c * PER_COND * GRID
        samples.append(square[at : at + GRID] + square[at + GRID : at + 2 * GRID] + square[at + 2 * GRID : at + 3 * GRID])
    inten = dot3_in(2, jnp.concatenate(samples, axis=0), tab["inter_cols"])
    inten = jnp.concatenate([inten[GRID * c : GRID * (c + 1)] for c in range(CONDS)], axis=1)
    inten = dot(tab["inter_rows"][...], stacked3(inten))
    slopes = []
    for c in range(CONDS):
        scale = kk[c // OWN, SLABS, c % OWN : c % OWN + 1] * (STEEP / (KERNELS * BAND * BAND))
        arg = scale * inten[:, TILE * c : TILE * (c + 1)] - STEEP * THRESH
        e = jnp.exp(-jnp.abs(arg))
        inverse = 1.0 / (1.0 + e)
        resist = jnp.where(arg >= 0, inverse, e * inverse)
        slopes.append((resist - goal) * (e * inverse * inverse) * (4.0 * scale))
    back = dot(tab["inter_rows_t"][...], stacked3(jnp.concatenate(slopes, axis=1)))
    back = jnp.concatenate([back[:, TILE * c : TILE * (c + 1)] for c in range(CONDS)], axis=0)
    weight = dot3_in(2, back, tab["inter_cols_t"])
    pulled = []
    for j in range(CONDS * PER_COND):
        at = j // PER_COND * GRID
        w = weight[at : at + GRID]
        pulled.append(field[GRID * j : GRID * (j + 1)] * jnp.concatenate([w, w], axis=1))
    pulled = dot3_in(2, jnp.concatenate(pulled, axis=0), tab["field_cols_t"])
    pulled = jnp.concatenate(
        [
            jnp.concatenate([pulled[GRID * j : GRID * (j + 1), TILE * p : TILE * (p + 1)] for j in range(CONDS * PER_COND)], axis=1)
            for p in range(2)
        ],
        axis=0,
    )
    pulled = dot(tab["field_rows_t"][...], stacked3(pulled))
    d_re = d_im = None
    for j in range(CONDS * PER_COND):
        k_re, k_im = kernel_tile(j)
        p_re = pulled[:BAND, TILE * j : TILE * (j + 1)]
        p_im = pulled[BAND:, TILE * j : TILE * (j + 1)]
        re, im = k_re * p_re + k_im * p_im, k_re * p_im - k_im * p_re
        d_re, d_im = (re, im) if d_re is None else (d_re + re, d_im + im)
    last = dot3(jnp.concatenate([d_re, d_im], axis=1), tab["last_cols"])
    out_ref[...] = stacked3(jnp.concatenate([last[:, :TILE], last[:, TILE:]], axis=0))
    share.wait_send()


def last_kernel(table_ref, sums_ref, out_ref):
    out_ref[...] = dot(table_ref[...], sums_ref[...])


def shards(mask, target, cond_index, kernels, dose):
    any_spec = pl.BlockSpec(memory_space=pl.ANY)
    vmem = pl.BlockSpec(memory_space=pltpu.VMEM)
    tables = [jnp.asarray(TABLES[name]) for name in NAMES]
    by_kernel = jnp.transpose(kernels, (0, 2, 1, 3))
    handed = pl.pallas_call(
        main_kernel,
        out_shape=[pltpu.VMEM(tables[-1].shape, BF), pltpu.VMEM((6 * BAND, TILE), BF)],
        in_specs=[any_spec] * (5 + len(tables)),
        out_specs=[vmem, vmem],
        scratch_shapes=[pltpu.VMEM(x.shape, x.dtype) for x in tables[:-1]]
        + [
            pltpu.VMEM(mask.shape, F32),
            pltpu.VMEM(target.shape, jnp.int32),
            pltpu.VMEM(by_kernel.shape, F32),
            pltpu.SMEM(cond_index.shape, jnp.int32),
            pltpu.SMEM(dose.shape, F32),
            pltpu.VMEM((2, SLABS + 1, BAND, TILE), F32),
            pltpu.VMEM((len(OFFSETS), PACK, TILE), F32),
            pltpu.VMEM((len(OFFSETS), PACK, TILE), F32),
            pltpu.SemaphoreType.DMA((len(tables) + 5,)),
            pltpu.SemaphoreType.DMA((2 * len(OFFSETS) + 1,)),
            pltpu.SemaphoreType.DMA((len(OFFSETS) + 1,)),
        ],
        compiler_params=pltpu.CompilerParams(
            collective_id=0, has_side_effects=True, vmem_limit_bytes=63 * 1024 * 1024
        ),
        name="spectra_and_gradient",
    )(mask, target, by_kernel, cond_index, dose, *tables)
    return pl.pallas_call(
        last_kernel,
        out_shape=jax.ShapeDtypeStruct(mask.shape, F32),
        in_specs=[vmem, vmem],
        out_specs=vmem,
        name="to_pixels",
    )(*[pltpu.with_memory_space_constraint(x, pltpu.VMEM) for x in handed])


def solution(mesh):
    in_specs = (P("row", "col"), P("row", "col"), P("cond"), P(), P())
    out_specs = P("row", "col")
    return jax.shard_map(shards, mesh=mesh, in_specs=in_specs, out_specs=out_specs, check_vma=False)
```

```python
import functools
import math

import jax
import jax.numpy as jnp
import ml_dtypes
import numpy as np
from jax import lax
from jax.experimental import pallas as pl
from jax.experimental.pallas import tpu as pltpu
from jax.sharding import PartitionSpec as P

MESH = pl.DeviceIdType.MESH
BF = jnp.bfloat16
F32 = jnp.float32

TILE = 128
MARGIN = 128
WINDOW = TILE + 2 * MARGIN
BAND = 24
KERNELS = 12
HALF = BAND // 2
REAL = 2 * HALF + 1
PACK = 5
GRID = 48
GROUP = 4
CONDS = 4
OWN = 2
PER_COND = KERNELS // GROUP
SLABS = 2 * OWN * PER_COND
STEEP = 4.0
THRESH = 0.6
OFFSETS = [(-1, -1), (-1, 1), (0, -1), (-1, 0), (1, 0), (0, 1), (1, -1), (1, 1)]
ORDER = [(0, 6, 2), (1, 7, 5), (3, 4)]
ARRIVAL = [3, 4, 5, 1, 7, 2, 0, 6]
FREQ = np.arange(BAND) - HALF
UNIT = 2.0 * math.pi / WINDOW


def parts(table):
    high = table.astype(ml_dtypes.bfloat16)
    low = (table - high.astype(np.float64)).astype(ml_dtypes.bfloat16)
    return high, low


def left3(table):
    high, low = parts(table)
    return np.concatenate([high, high, low], axis=1)


def pair(table):
    return np.stack(parts(table))


def real_basis(positions):
    order = np.arange(HALF + 1)[:, None] * positions[None, :] % WINDOW * UNIT
    return np.concatenate([np.cos(order), np.sin(order)[1:]], axis=0)


def make_tables():
    t = {}
    pixels = np.arange(TILE)
    rows = np.zeros((3, PACK, 8, TILE))
    cols = np.zeros((3, TILE, TILE))
    for d in range(3):
        basis = real_basis(pixels + TILE * (d - 1))
        rows[d, :, :PACK] = basis.reshape(PACK, PACK, TILE)
        for j in range(PACK):
            cols[d, :, REAL * j : REAL * (j + 1)] = basis.T / WINDOW
    t["dft_rows"] = pair(np.pad(rows.reshape(3 * PACK * 8, TILE), ((0, 8), (0, 0))))
    for d in range(3):
        t[f"dft_cols{d}"] = pair(cols[d])

    pick = np.zeros((PACK, BAND, 2 * TILE), np.float32)
    spread = np.zeros((2, TILE, 2, GROUP, 32))
    for row, f in enumerate(FREQ):
        a = abs(f)
        j, i = divmod(a, PACK)
        pick[i, row, REAL * j : REAL * (j + 1)] = 1.0
        if f:
            j, i = divmod(HALF + a, PACK)
            pick[i, row, TILE + REAL * j : TILE + REAL * (j + 1)] = np.sign(f)
    for j in range(PACK):
        for col, g in enumerate(FREQ):
            cos_at = REAL * j + abs(g)
            spread[0, cos_at, 0, :, col] = 1.0
            spread[1, cos_at, 1, :, col] = -1.0
            if g:
                sin_at = REAL * j + HALF + abs(g)
                spread[1, sin_at, 0, :, col] = -np.sign(g)
                spread[0, sin_at, 1, :, col] = -np.sign(g)
    t["pick"] = pick
    t["spread"] = spread.reshape(2 * TILE, 2 * TILE).astype(ml_dtypes.bfloat16)

    rows_of = np.zeros((BAND, BAND * BAND), np.float32)
    fold = np.zeros((BAND * BAND, GROUP, 32))
    for l in range(BAND * BAND):
        rows_of[l // BAND, l] = 1.0
        fold[l, :, l % BAND] = 1.0
    t["rows_of"] = rows_of
    t["fold"] = fold.reshape(BAND * BAND, TILE).astype(ml_dtypes.bfloat16)

    angle = FREQ[:, None] * np.arange(GRID)[None, :] % GRID * (2.0 * math.pi / GRID)
    c, s = np.cos(angle), np.sin(angle)
    field_rows = np.block([[c.T, -s.T], [s.T, c.T]])
    t["field_rows"] = left3(field_rows)
    t["field_rows_t"] = left3(field_rows.T)
    field_cols = np.zeros((2, GROUP, 32, 2, GROUP, 64))
    for k in range(GROUP):
        field_cols[0, k, :BAND, 0, k, :GRID] = c
        field_cols[1, k, :BAND, 0, k, :GRID] = -s
        field_cols[0, k, :BAND, 1, k, :GRID] = s
        field_cols[1, k, :BAND, 1, k, :GRID] = c
    field_cols = field_cols.reshape(2 * TILE, 4 * TILE)
    t["field_cols"] = pair(field_cols)
    t["field_cols_t"] = pair(field_cols.T.copy())

    step = WINDOW // GRID
    gap = pixels[:, None] - step * np.arange(GRID)[None, :]
    orders = np.arange(1, GRID // 2)
    inter = (1.0 + 2.0 * np.cos(orders * gap[:, :, None] * UNIT).sum(-1)) / GRID
    inter_wide = np.zeros((TILE, GROUP, 64))
    inter_wide[:, :, :GRID] = inter[:, None, :]
    inter_wide = inter_wide.reshape(TILE, 2 * TILE)
    t["inter_rows"] = left3(inter)
    t["inter_rows_t"] = left3(inter.T)
    t["inter_cols"] = pair(inter_wide.T.copy())
    t["inter_cols_t"] = pair(inter_wide)

    turn = FREQ[:, None] * pixels[None, :] % WINDOW * UNIT
    c, s = np.cos(turn), np.sin(turn)
    last_cols = np.zeros((2, GROUP, 32, 2, TILE))
    last_cols[0, :, :BAND, 0] = c / WINDOW
    last_cols[1, :, :BAND, 0] = -s / WINDOW
    last_cols[0, :, :BAND, 1] = -s / WINDOW
    last_cols[1, :, :BAND, 1] = -c / WINDOW
    t["last_cols"] = pair(last_cols.reshape(2 * TILE, 2 * TILE))
    t["last_rows"] = left3(np.concatenate([c, s], axis=0).T)
    return t


TABLES = make_tables()
NAMES = [
    "dft_rows", "dft_cols0", "dft_cols2", "dft_cols1", "rows_of", "fold", "pick", "spread", "field_rows", "field_cols",
    "inter_cols", "inter_rows", "inter_rows_t", "inter_cols_t", "field_cols_t", "field_rows_t", "last_cols",
    "last_rows",
]

LOADS = ("kernels", "cond", "dose", "rows_of", "fold")


def split(x):
    high = x.astype(BF)
    return high, (x - high.astype(F32)).astype(BF)


def dot(a, b):
    return jnp.dot(a, b, preferred_element_type=F32)


def dot3(x, table):
    high, low = split(x)
    return dot(high, table[0]) + dot(low, table[0]) + dot(high, table[1])


def dot3_in(pieces, x, table):
    rows = x.shape[0] // pieces
    return jnp.concatenate([dot3(x[rows * i : rows * (i + 1)], table) for i in range(pieces)], axis=0)


def stacked3(x):
    high, low = split(x)
    return jnp.concatenate([high, low, high], axis=0)


def main_kernel(*refs):
    n = len(NAMES)
    mask_hbm, target_hbm, kernels_hbm, cond_hbm, dose_hbm = refs[:5]
    tables_hbm = refs[5 : 5 + n]
    table_ref, out_ref = refs[5 + n : 7 + n]
    scratch = refs[7 + n :]
    tab = dict(zip(NAMES, list(scratch[: n - 1]) + [table_ref]))
    mask, target, kernels, cond_ref, dose_ref, kk, sent, held, load_sem, send_sem, recv_sem = scratch[n - 1 :]

    row, col, core = (lax.axis_index(a) for a in ("row", "col", "cond"))
    n_row, n_col = lax.axis_size("row"), lax.axis_size("col")

    copies = {}
    first = [("mask", mask_hbm, mask)] + [(m, s, tab[m]) for m, s in zip(NAMES[:4], tables_hbm[:4])]
    later = (
        [("kernels", kernels_hbm, kernels), ("cond", cond_hbm, cond_ref), ("dose", dose_hbm, dose_ref)]
        + [(m, s, tab[m]) for m, s in zip(NAMES[4:], tables_hbm[4:])]
        + [("target", target_hbm, target)]
    )
    for i, (name, src, dst) in enumerate(first + later):
        copies[name] = pltpu.make_async_copy(src, dst, load_sem.at[i])
    for name, _, _ in first:
        copies[name].start()

    held[...] = jnp.zeros_like(held)
    even = lax.rem(col, 2) == 0

    def from_core(dr, dc, at_row, at_col, at_core):
        return jnp.where((at_row == 0) & (at_col == 0) & (at_core == 0), 0, 1) if dc else 0

    barrier = pltpu.get_barrier_semaphore()
    pl.semaphore_signal(barrier, inc=1, device_id=(row, col, 1 - core), device_id_type=MESH)
    there = []
    count = jnp.int32(1)
    for dr, dc in OFFSETS:
        ok = (row + dr >= 0) & (row + dr < n_row) & (col + dc >= 0) & (col + dc < n_col)
        there.append(ok)
        for to in range(2):
            count = count + jnp.where(ok & (core == from_core(dr, dc, row + dr, col + dc, to)), 1, 0)
        sender = from_core(dr, dc, row, col, core)

        @pl.when(ok)
        def _():
            pl.semaphore_signal(barrier, inc=1, device_id=(row + dr, col + dc, sender), device_id_type=MESH)

    def sending(i, to):
        dr, dc = OFFSETS[i]
        return there[len(OFFSETS) - 1 - i] & (core == from_core(dr, dc, row - dr, col - dc, to))

    goes = {(i, to): sending(i, to) for i in range(len(OFFSETS)) for to in range(2)}

    for name in ("mask", "dft_rows"):
        copies[name].wait()
    lanes = lax.broadcasted_iota(jnp.int32, (8, TILE), 1)
    table = tab["dft_rows"]
    partial = dot(jnp.concatenate([table[0], table[0], table[1]], axis=1), stacked3(mask[...]))
    partial = split(partial)

    def blocks_of(e):
        copies[f"dft_cols{e}"].wait()
        table = tab[f"dft_cols{e}"]
        products = dot(partial[0], table[0]) + dot(partial[1], table[0]) + dot(partial[0], table[1])
        own = None
        for d in range(3):
            block = None
            for j in range(PACK):
                piece = products[8 * (PACK * d + j) : 8 * (PACK * d + j + 1)]
                block = piece if block is None else jnp.where(lanes < REAL * j, block, piece)
            if d == 1 and e == 1:
                own = block
            else:
                sent[OFFSETS.index((d - 1, e - 1))] = block[:PACK]
        return own

    sends = {}

    def send(order):
        for i in order:
            dr, dc = OFFSETS[i]
            for to in range(2):
                sends[i, to] = pltpu.make_async_remote_copy(
                    src_ref=sent.at[i],
                    dst_ref=held.at[i],
                    send_sem=send_sem.at[2 * i + to],
                    recv_sem=recv_sem.at[i],
                    device_id=(row - dr, col - dc, to),
                    device_id_type=MESH,
                )

                @pl.when(goes[i, to])
                def _():
                    sends[i, to].start()

    blocks_of(0)
    lane = lax.broadcasted_iota(jnp.int32, (BAND, TILE), 1) // 32

    def arrange(step, carry):
        c = step // PER_COND
        group = step - PER_COND * c
        setting = cond_ref[c]
        lines = [kernels[setting, group * GROUP + k, part : part + 1, :] for part in range(2) for k in range(GROUP)]
        folded = []
        for half in (lines[:GROUP], lines[GROUP:]):
            high, low = split(jnp.concatenate([line * tab["rows_of"][...] for line in half], axis=0))
            folded.append(dot(high, tab["fold"][...]) + dot(low, tab["fold"][...]))
        for part in range(2):
            total = folded[part][:BAND]
            for k in range(1, GROUP):
                total = jnp.where(lane == k, folded[part][BAND * k : BAND * (k + 1)], total)
            kk[0, OWN * PER_COND * part + step] = total
        return carry

    def arrange_all():
        for name, _, _ in later:
            copies[name].start()
        for name in LOADS:
            copies[name].wait()
        for c in range(OWN):
            kk[0, SLABS, c : c + 1] = jnp.full((1, TILE), dose_ref[cond_ref[c]], F32)
        lax.fori_loop(0, OWN * PER_COND, arrange, 0)

    ahead = even & ((row > 0) | (col > 0) | (core > 0))
    pl.when(ahead)(arrange_all)

    pl.semaphore_wait(barrier, count)
    send(ORDER[0])
    blocks_of(2)
    send(ORDER[1])
    own = blocks_of(1)
    send(ORDER[2])

    pl.when(jnp.logical_not(ahead))(arrange_all)
    share = pltpu.make_async_remote_copy(
        src_ref=kk.at[0],
        dst_ref=kk.at[1],
        send_sem=send_sem.at[2 * len(OFFSETS)],
        recv_sem=recv_sem.at[len(OFFSETS)],
        device_id=(row, col, 1 - core),
        device_id_type=MESH,
    )
    share.start()

    for name in NAMES[6:] + ["target"]:
        copies[name].wait()
    share.wait_recv()
    goal = target[...].astype(F32)

    for i in range(len(OFFSETS)):
        for to in range(2):

            @pl.when(goes[i, to])
            def _(i=i, to=to):
                sends[i, to].wait_send()

    z = own[:PACK]
    for i in ARRIVAL:

        @pl.when(there[i])
        def _(i=i):
            sends[i, 0].wait_recv()

        z = z + held[i]
    chosen = None
    for i in range(PACK):
        line = jnp.concatenate([z[i : i + 1], z[i : i + 1]], axis=1)
        piece = line * tab["pick"][i]
        chosen = piece if chosen is None else chosen + piece
    high, low = split(chosen)
    spectrum = dot(high, tab["spread"][...]) + dot(low, tab["spread"][...])
    s_re, s_im = spectrum[:, :TILE], spectrum[:, TILE:]

    def kernel_tile(j):
        who, at = divmod(j, OWN * PER_COND)
        return kk[who, at], kk[who, OWN * PER_COND + at]

    product = []
    for j in range(CONDS * PER_COND):
        k_re, k_im = kernel_tile(j)
        product.append(jnp.concatenate([k_re * s_re - k_im * s_im, k_re * s_im + k_im * s_re], axis=0))
    along = dot(tab["field_rows"][...], stacked3(jnp.concatenate(product, axis=1)))
    along = jnp.concatenate(
        [
            jnp.concatenate([along[:GRID, TILE * j : TILE * (j + 1)], along[GRID:, TILE * j : TILE * (j + 1)]], axis=1)
            for j in range(CONDS * PER_COND)
        ],
        axis=0,
    )
    field = dot3(along, tab["field_cols"])
    square = field * field
    square = square[:, : 2 * TILE] + square[:, 2 * TILE :]
    samples = []
    for c in range(CONDS):
        at = c * PER_COND * GRID
        samples.append(square[at : at + GRID] + square[at + GRID : at + 2 * GRID] + square[at + 2 * GRID : at + 3 * GRID])
    inten = dot3_in(2, jnp.concatenate(samples, axis=0), tab["inter_cols"])
    inten = jnp.concatenate([inten[GRID * c : GRID * (c + 1)] for c in range(CONDS)], axis=1)
    inten = dot(tab["inter_rows"][...], stacked3(inten))
    slopes = []
    for c in range(CONDS):
        scale = kk[c // OWN, SLABS, c % OWN : c % OWN + 1] * (STEEP / (KERNELS * BAND * BAND))
        arg = scale * inten[:, TILE * c : TILE * (c + 1)] - STEEP * THRESH
        e = jnp.exp(-jnp.abs(arg))
        inverse = 1.0 / (1.0 + e)
        resist = jnp.where(arg >= 0, inverse, e * inverse)
        slopes.append((resist - goal) * (e * inverse * inverse) * (4.0 * scale))
    back = dot(tab["inter_rows_t"][...], stacked3(jnp.concatenate(slopes, axis=1)))
    back = jnp.concatenate([back[:, TILE * c : TILE * (c + 1)] for c in range(CONDS)], axis=0)
    weight = dot3_in(2, back, tab["inter_cols_t"])
    pulled = []
    for j in range(CONDS * PER_COND):
        at = j // PER_COND * GRID
        w = weight[at : at + GRID]
        pulled.append(field[GRID * j : GRID * (j + 1)] * jnp.concatenate([w, w], axis=1))
    pulled = dot3_in(2, jnp.concatenate(pulled, axis=0), tab["field_cols_t"])
    pulled = jnp.concatenate(
        [
            jnp.concatenate([pulled[GRID * j : GRID * (j + 1), TILE * p : TILE * (p + 1)] for j in range(CONDS * PER_COND)], axis=1)
            for p in range(2)
        ],
        axis=0,
    )
    pulled = dot(tab["field_rows_t"][...], stacked3(pulled))
    d_re = d_im = None
    for j in range(CONDS * PER_COND):
        k_re, k_im = kernel_tile(j)
        p_re = pulled[:BAND, TILE * j : TILE * (j + 1)]
        p_im = pulled[BAND:, TILE * j : TILE * (j + 1)]
        re, im = k_re * p_re + k_im * p_im, k_re * p_im - k_im * p_re
        d_re, d_im = (re, im) if d_re is None else (d_re + re, d_im + im)
    last = dot3(jnp.concatenate([d_re, d_im], axis=1), tab["last_cols"])
    out_ref[...] = stacked3(jnp.concatenate([last[:, :TILE], last[:, TILE:]], axis=0))
    share.wait_send()


def last_kernel(table_ref, sums_ref, out_ref):
    out_ref[...] = dot(table_ref[...], sums_ref[...])


def shards(mask, target, cond_index, kernels, dose):
    any_spec = pl.BlockSpec(memory_space=pl.ANY)
    vmem = pl.BlockSpec(memory_space=pltpu.VMEM)
    tables = [jnp.asarray(TABLES[name]) for name in NAMES]
    by_kernel = jnp.transpose(kernels, (0, 2, 1, 3))
    handed = pl.pallas_call(
        main_kernel,
        out_shape=[pltpu.VMEM(tables[-1].shape, BF), pltpu.VMEM((6 * BAND, TILE), BF)],
        in_specs=[any_spec] * (5 + len(tables)),
        out_specs=[vmem, vmem],
        scratch_shapes=[pltpu.VMEM(x.shape, x.dtype) for x in tables[:-1]]
        + [
            pltpu.VMEM(mask.shape, F32),
            pltpu.VMEM(target.shape, jnp.int32),
            pltpu.VMEM(by_kernel.shape, F32),
            pltpu.SMEM(cond_index.shape, jnp.int32),
            pltpu.SMEM(dose.shape, F32),
            pltpu.VMEM((2, SLABS + 1, BAND, TILE), F32),
            pltpu.VMEM((len(OFFSETS), PACK, TILE), F32),
            pltpu.VMEM((len(OFFSETS), PACK, TILE), F32),
            pltpu.SemaphoreType.DMA((len(tables) + 5,)),
            pltpu.SemaphoreType.DMA((2 * len(OFFSETS) + 1,)),
            pltpu.SemaphoreType.DMA((len(OFFSETS) + 1,)),
        ],
        compiler_params=pltpu.CompilerParams(
            collective_id=0, has_side_effects=True, vmem_limit_bytes=63 * 1024 * 1024
        ),
        name="spectra_and_gradient",
    )(mask, target, by_kernel, cond_index, dose, *tables)
    return pl.pallas_call(
        last_kernel,
        out_shape=jax.ShapeDtypeStruct(mask.shape, F32),
        in_specs=[vmem, vmem],
        out_specs=vmem,
        name="to_pixels",
    )(*[pltpu.with_memory_space_constraint(x, pltpu.VMEM) for x in handed])


def solution(mesh):
    in_specs = (P("row", "col"), P("row", "col"), P("cond"), P(), P())
    out_specs = P("row", "col")
    return jax.shard_map(shards, mesh=mesh, in_specs=in_specs, out_specs=out_specs, check_vma=False)
```
